32 devices in a mesh: seq: 8 (over y, x, core), tp: 4 (over z).
Axes of the slice: x: 2, y: 2, z: 4, core: 2. Of those that a mesh axis runs over, the one named last changes fastest.
Arguments:
- hidden_in: bfloat16 [2, 2048, 2048], P(None, ('seq', 'tp')), may hold values from -6 to 6
- output_grad: bfloat16 [2, 2048, 2048], P(None, ('seq', 'tp')), may hold values from -6 to 6
- document_lengths: int32 [2, 4], replicated, may hold values from 1 to 2047, as said below
- attention_gain: float32 [2048], replicated, may hold values from 0.5 to 1.5
- query_weight: bfloat16 [2048, 2048], P(None, 'tp'), may hold values from -0.125 to 0.125
- key_weight: bfloat16 [2048, 1024], P(None, 'tp'), may hold values from -0.125 to 0.125
- value_weight: bfloat16 [2048, 1024], P(None, 'tp'), may hold values from -0.125 to 0.125
- query_gain: float32 [128], replicated, may hold values from 0.5 to 1.5
- key_gain: float32 [128], replicated, may hold values from 0.5 to 1.5
- output_weight: bfloat16 [2048, 2048], P('tp'), may hold values from -0.5 to 0.5
- feedforward_gain: float32 [2048], replicated, may hold values from 0.5 to 1.5
- gate_weight: bfloat16 [2048, 6144], P(None, 'tp'), may hold values from -0.125 to 0.125
- up_weight: bfloat16 [2048, 6144], P(None, 'tp'), may hold values from -0.125 to 0.125
- down_weight: bfloat16 [6144, 2048], P('tp'), may hold values from -0.078125 to 0.078125
Outputs:
- block_out: bfloat16 [2, 2048, 2048], P(None, ('seq', 'tp'))
- input_grad: float32 [2, 2048, 2048], P(None, ('seq', 'tp'))
- attention_gain_grad: float32 [2048], replicated
- query_weight_grad: float32 [2048, 2048], P(None, 'tp')
- key_weight_grad: float32 [2048, 1024], P(None, 'tp')
- value_weight_grad: float32 [2048, 1024], P(None, 'tp')
- query_gain_grad: float32 [128], replicated
- key_gain_grad: float32 [128], replicated
- output_weight_grad: float32 [2048, 2048], P('tp')
- feedforward_gain_grad: float32 [2048], replicated
- gate_weight_grad: float32 [2048, 6144], P(None, 'tp')
- up_weight_grad: float32 [2048, 6144], P(None, 'tp')
- down_weight_grad: float32 [6144, 2048], P('tp')
The draws below stay inside these ranges and needn't reach their ends.
Inputs may be any that keep to these rules, and one draw needn't show every extreme that they name: `document_lengths`: each row holds four documents, lengths summing to 2048; in one row, drawn from the seed, a document starts within the first 256 positions and ends within the last 256.
All inputs are finite; a program needn't handle non-finite values.
Results may differ from the reference program's by a relative error of at most 0.02.
Values may be sent and summed in bfloat16 or wider, within the bound.
No kernel may reach another device: no remote copies, remote signals or barrier semaphores. Data moves between devices by JAX's collectives and lax.ppermute only.
A program may use at most 192 MiB of HBM per device.

```python
import math
import jax
import jax.numpy as jnp
from jax import lax

D = 2048
HEADS = 16
KV_HEADS = 8
HEAD = 128
FF = 6144
SPAN = 256
ROWS = 2
ROW_LEN = 2048


def draw_document_lengths(key, part):
    key = jax.random.fold_in(key, 7)
    key_list = jax.random.split(key, 7)
    third_len = ROW_LEN // 3
    first_cut = jax.random.randint(key_list[0], (ROWS,), 1, third_len)
    second_cut = jax.random.randint(key_list[1], (ROWS,), third_len, 2 * third_len)
    third_cut = jax.random.randint(key_list[2], (ROWS,), 2 * third_len, ROW_LEN)
    long_first = jax.random.randint(key_list[3], (ROWS,), 1, SPAN)
    long_second = jax.random.randint(key_list[4], (ROWS,), ROW_LEN - SPAN + 1, ROW_LEN - 1)
    long_third = jax.random.randint(key_list[5], (ROWS,), long_second + 1, ROW_LEN)
    chosen = jax.random.randint(key_list[6], (), 0, ROWS)
    picked = jnp.arange(ROWS, dtype=jnp.int32) == chosen
    cut_one = jnp.where(picked, long_first, first_cut)
    cut_two = jnp.where(picked, long_second, second_cut)
    cut_three = jnp.where(picked, long_third, third_cut)
    bounds = jnp.stack([jnp.zeros((ROWS,), jnp.int32), cut_one, cut_two, cut_three, jnp.full((ROWS,), ROW_LEN, jnp.int32)], axis=1)
    return (bounds[:, 1:] - bounds[:, :-1]).astype(jnp.int32)


def block_levels(own_key, dims, pieces, low, high):
    level = 1.0
    for position, blocks in pieces:
        steps = jax.random.uniform(jax.random.fold_in(jax.random.fold_in(own_key, 6), position), (blocks,), jnp.float32, low / len(pieces), high / len(pieces))
        level = level * jnp.repeat(jnp.exp(steps), dims[position] // blocks).reshape((-1,) + (1,) * (len(dims) - 1 - position))
    return level


def bell_draw(own_key, dims, spread, bound, cuts=(), held_as=jnp.bfloat16):
    level = block_levels(own_key, dims, cuts, -0.22, 0.18) if cuts else 1.0
    entries = jax.random.normal(own_key, dims, jnp.float32) * spread * level
    return jnp.minimum(jnp.maximum(entries, -bound), bound).astype(held_as)


def setup_inputs(seed: int = 0) -> dict:
    arg_keys = jax.random.split(jax.random.key(seed), 15)
    return {
        "hidden_in": bell_draw(arg_keys[0], (ROWS, ROW_LEN, D), 1.0, 6.0, ((1, 32),)),
        "output_grad": bell_draw(arg_keys[1], (ROWS, ROW_LEN, D), 1.0, 6.0, ((1, 32),)),
        "document_lengths": draw_document_lengths(jax.random.fold_in(arg_keys[14], 71), 0),
        "attention_gain": jnp.clip(1.0 + 0.1 * jax.random.normal(arg_keys[3], (D,), jnp.float32), 0.5, 1.5),
        "query_weight": bell_draw(arg_keys[4], (D, HEADS * HEAD), D ** -0.5, 0.125, ((1, 4),)),
        "key_weight": bell_draw(arg_keys[5], (D, KV_HEADS * HEAD), D ** -0.5, 0.125, ((1, 4),)),
        "value_weight": bell_draw(arg_keys[6], (D, KV_HEADS * HEAD), D ** -0.5, 0.125, ((1, 4),)),
        "query_gain": jnp.clip(1.0 + 0.1 * jax.random.normal(arg_keys[7], (HEAD,), jnp.float32), 0.5, 1.5),
        "key_gain": jnp.clip(1.0 + 0.1 * jax.random.normal(arg_keys[8], (HEAD,), jnp.float32), 0.5, 1.5),
        "output_weight": bell_draw(arg_keys[9], (HEADS * HEAD, D), (HEADS * HEAD // 16) ** -0.5, 0.5, ((0, 4),)),
        "feedforward_gain": jnp.clip(1.0 + 0.1 * jax.random.normal(arg_keys[10], (D,), jnp.float32), 0.5, 1.5),
        "gate_weight": bell_draw(arg_keys[11], (D, FF), D ** -0.5, 0.125, ((1, 4),)),
        "up_weight": bell_draw(arg_keys[12], (D, FF), D ** -0.5, 0.125, ((1, 4),)),
        "down_weight": bell_draw(arg_keys[13], (FF, D), FF ** -0.5, 0.078125, ((0, 4),)),
    }


@jax.custom_vjp
def low(v):
    return lax.optimization_barrier(v.astype(jnp.bfloat16)).astype(jnp.float32)

@jax.custom_vjp
def low_back(v):
    return v

def low_keep(v):
    return (low(v), None)

def low_pass(kept, grad):
    return (grad,)

def back_keep(v):
    return (v, None)

def back_low(kept, grad):
    return (low(grad),)
low.defvjp(low_keep, low_pass)
low_back.defvjp(back_keep, back_low)
epsilon = 1e-06
rope_base = 1000000.0
masked_score = -1e+30

def doc_tables(document_lengths, length):
    doc_ends = jnp.cumsum(document_lengths, axis=1)
    doc_starts = doc_ends - document_lengths
    places = jnp.arange(length, dtype=jnp.int32)
    segment = lax.optimization_barrier(jnp.sum((places[None, :, None] >= doc_ends[:, None, :]).astype(jnp.int32), axis=2))
    numbers = jnp.arange(document_lengths.shape[1], dtype=jnp.int32)
    owned_by = segment[:, :, None] == numbers[None, None, :]
    doc_begin = lax.optimization_barrier(jnp.sum(jnp.where(owned_by, doc_starts[:, None, :], 0), axis=2))
    return (segment, places[None, :] - doc_begin)

def rope_tables(within, head_size):
    half_size = head_size // 2
    frequency = rope_base ** (-2.0 * jnp.arange(half_size, dtype=jnp.float32) / head_size)
    angles = within.astype(jnp.float32)[..., None] * frequency
    return (jnp.cos(angles)[:, :, None, :], jnp.sin(angles)[:, :, None, :])

def rotate(values, cos_table, sin_table):
    half_size = values.shape[-1] // 2
    front_half = values[..., :half_size]
    back_half = values[..., half_size:]
    return jnp.concatenate([front_half * cos_table - back_half * sin_table, back_half * cos_table + front_half * sin_table], axis=-1)

def rms_norm(values, gain_vec):
    return values * lax.rsqrt(lax.optimization_barrier(jnp.mean(values * values, axis=-1, keepdims=True)) + epsilon) * gain_vec

def matmul(left_side, right_side):
    return jnp.einsum('...d,de->...e', left_side, right_side, precision=lax.Precision.HIGHEST)

def attend(queries, keys_roped, values, segment, scale_by):
    row_count, row_length, head_count, head_size = queries.shape
    key_heads = keys_roped.shape[2]
    group_size = head_count // key_heads
    block_rows = math.gcd(row_length, 512)
    block_count = row_length // block_rows
    places = jnp.arange(row_length, dtype=jnp.int32)

    def row_fn(row_items):
        query_row, key_row, value_row, segment_row = row_items
        query_blocks = query_row.reshape(block_count, block_rows, key_heads, group_size, head_size)
        block_starts = jnp.arange(block_count, dtype=jnp.int32) * block_rows

        def block_fn(block_items):
            query_block, block_start = block_items
            query_places = block_start + jnp.arange(block_rows, dtype=jnp.int32)
            query_segment = lax.dynamic_slice_in_dim(segment_row, block_start, block_rows, 0)
            allowed = (places[None, :] <= query_places[:, None]) & (segment_row[None, :] == query_segment[:, None])
            scores = low_back(jnp.einsum('qkgd,lkd->kgql', query_block, key_row, precision=lax.Precision.HIGHEST) * scale_by)
            scores = jnp.where(allowed[None, None], scores, masked_score)
            probability = low(jax.nn.softmax(scores, axis=-1))
            attended = jnp.einsum('kgql,lkd->qkgd', probability, value_row, precision=lax.Precision.HIGHEST)
            return attended.reshape(block_rows, head_count * head_size)
        outputs = lax.map(jax.checkpoint(block_fn), (query_blocks, block_starts))
        return outputs.reshape(row_length, head_count * head_size)
    return lax.map(row_fn, (queries, keys_roped, values, segment))

def reference(hidden_in, output_grad, document_lengths, attention_gain, query_weight, key_weight, value_weight, query_gain, key_gain, output_weight, feedforward_gain, gate_weight, up_weight, down_weight):
    row_count, row_length, model_width = hidden_in.shape
    segment, within = doc_tables(document_lengths, row_length)
    cos_table, sin_table = rope_tables(within, HEAD)
    scale_by = HEAD ** (-0.5)

    def forward(hidden, attn_gain, q_proj, k_proj, v_proj, q_norm, k_norm, o_proj, ff_gain, gate_proj, up_proj, down_proj):
        normed1 = low(rms_norm(hidden, attn_gain))
        query_raw = low_back(matmul(normed1, q_proj)).reshape(row_count, row_length, HEADS, HEAD)
        key_raw = low_back(matmul(normed1, k_proj)).reshape(row_count, row_length, KV_HEADS, HEAD)
        values = low(low_back(matmul(normed1, v_proj))).reshape(row_count, row_length, KV_HEADS, HEAD)
        queries = low(rotate(rms_norm(query_raw, q_norm), cos_table, sin_table))
        keys_roped = low(rotate(rms_norm(key_raw, k_norm), cos_table, sin_table))
        attended = attend(queries, keys_roped, values, segment, scale_by)
        attn_out = low_back(low(attended))
        middle = hidden + low_back(matmul(attn_out, o_proj))
        normed2 = low(rms_norm(middle, ff_gain))
        gate_act = low_back(matmul(normed2, gate_proj))
        up_act = low_back(matmul(normed2, up_proj))
        hidden_mid = low(jax.nn.silu(gate_act) * up_act)
        return middle + low_back(matmul(hidden_mid, down_proj))
    primals = (hidden_in.astype(jnp.float32), attention_gain.astype(jnp.float32), query_weight.astype(jnp.float32), key_weight.astype(jnp.float32), value_weight.astype(jnp.float32), query_gain.astype(jnp.float32), key_gain.astype(jnp.float32), output_weight.astype(jnp.float32), feedforward_gain.astype(jnp.float32), gate_weight.astype(jnp.float32), up_weight.astype(jnp.float32), down_weight.astype(jnp.float32))
    result, pullback = jax.vjp(forward, *primals)
    grads = pullback(output_grad.astype(jnp.float32))
    return (result.astype(jnp.bfloat16), grads[0], grads[1], grads[2], grads[3], grads[4], grads[5], grads[6], grads[7], grads[8], grads[9], grads[10], grads[11])
```

```python
import jax
import jax.numpy as jnp
from jax import lax
from jax.sharding import PartitionSpec as P

HEAD = 128


epsilon = 1e-06
rope_base = 1000000.0
masked_score = -1e30


def doc_tables(document_lengths, length):
    doc_ends = jnp.stack(
        [jnp.sum(document_lengths[:, : n + 1], axis=1) for n in range(document_lengths.shape[1])], axis=1
    )
    doc_starts = doc_ends - document_lengths
    places = jnp.arange(length, dtype=jnp.int32)
    segment = jnp.sum((places[None, :, None] >= doc_ends[:, None, :]).astype(jnp.int32), axis=2)
    numbers = jnp.arange(document_lengths.shape[1], dtype=jnp.int32)
    owned_by = segment[:, :, None] == numbers[None, None, :]
    doc_begin = jnp.sum(jnp.where(owned_by, doc_starts[:, None, :], 0), axis=2)
    return (segment, places[None, :] - doc_begin)


def rope_tables(within, head_size):
    half_size = head_size // 2
    frequency = rope_base ** (-2.0 * jnp.arange(half_size, dtype=jnp.float32) / head_size)
    angles = within.astype(jnp.float32)[..., None] * frequency
    return (jnp.cos(angles)[:, :, None, :], jnp.sin(angles)[:, :, None, :])


def rotate(values, cos_table, sin_table):
    half_size = values.shape[-1] // 2
    front_half = values[..., :half_size]
    back_half = values[..., half_size:]
    return jnp.concatenate(
        [
            front_half * cos_table - back_half * sin_table,
            back_half * cos_table + front_half * sin_table,
        ],
        axis=-1,
    )


def unrotate(upstream, cos_table, sin_table):
    half_size = upstream.shape[-1] // 2
    front_half = upstream[..., :half_size]
    back_half = upstream[..., half_size:]
    return jnp.concatenate(
        [
            front_half * cos_table + back_half * sin_table,
            back_half * cos_table - front_half * sin_table,
        ],
        axis=-1,
    )


def rms_forward(values, gain_vec):
    inverse = lax.rsqrt(jnp.mean(values * values, axis=-1, keepdims=True) + epsilon)
    return (values * inverse * gain_vec, inverse)


def rms_backward(values, inverse, gain_vec, upstream):
    scaled = upstream * gain_vec
    through = inverse * scaled - values * (inverse * inverse * inverse) * jnp.mean(
        values * scaled, axis=-1, keepdims=True
    )
    gain_grad = jnp.sum((upstream * values * inverse).reshape(-1, values.shape[-1]), axis=0)
    return (through, gain_grad)


def project(activations, weight_mat):
    return jnp.einsum("rcd,de->rce", activations, weight_mat, preferred_element_type=jnp.float32)


def project_back(grads_in, weight_mat):
    return jnp.einsum("rce,de->rcd", grads_in, weight_mat, preferred_element_type=jnp.float32)


def weight_grad(activations, grads_in):
    return jnp.einsum("rcd,rce->de", activations, grads_in, preferred_element_type=jnp.float32)


def attend_forward(queries, all_keys, all_values, allowed, scale_by):

    def one_row(row_items):
        query_row, key_row, value_row, mask_row = row_items
        scores = (
            jnp.einsum("qkgd,lkd->kgql", query_row, key_row, preferred_element_type=jnp.float32)
            * scale_by
        )
        scores = jnp.where(mask_row[None, None], scores, masked_score)
        row_top = jnp.max(scores, axis=-1, keepdims=True)
        powers = jnp.exp(scores - row_top)
        totals = jnp.sum(powers, axis=-1, keepdims=True)
        probability = (powers / totals).astype(jnp.bfloat16)
        attended = jnp.einsum(
            "kgql,lkd->qkgd", probability, value_row, preferred_element_type=jnp.float32
        )
        return (attended, (row_top + jnp.log(totals))[..., 0])

    return lax.map(one_row, (queries, all_keys, all_values, allowed))


def attend_backward(queries, all_keys, all_values, attn_grad, log_sums, allowed, scale_by):

    def one_row(row_items):
        query_row, key_row, value_row, grad_row, lse_row, mask_row = row_items
        scores = (
            jnp.einsum("qkgd,lkd->kgql", query_row, key_row, preferred_element_type=jnp.float32)
            * scale_by
        )
        probability = jnp.where(mask_row[None, None], jnp.exp(scores - lse_row[..., None]), 0.0)
        prob_grad = jnp.einsum(
            "qkgd,lkd->kgql", grad_row, value_row, preferred_element_type=jnp.float32
        )
        centre = jnp.sum(probability * prob_grad, axis=-1, keepdims=True)
        score_grad = (probability * (prob_grad - centre)).astype(jnp.bfloat16)
        query_grad = (
            jnp.einsum("kgql,lkd->qkgd", score_grad, key_row, preferred_element_type=jnp.float32)
            * scale_by
        )
        key_grad = (
            jnp.einsum("kgql,qkgd->lkd", score_grad, query_row, preferred_element_type=jnp.float32)
            * scale_by
        )
        value_grad = jnp.einsum(
            "kgql,qkgd->lkd",
            probability.astype(jnp.bfloat16),
            grad_row,
            preferred_element_type=jnp.float32,
        )
        return (query_grad, key_grad, value_grad)

    return lax.map(one_row, (queries, all_keys, all_values, attn_grad, log_sums, allowed))


def body(
    hidden_in,
    output_grad,
    document_lengths,
    attention_gain,
    query_weight,
    key_weight,
    value_weight,
    query_gain,
    key_gain,
    output_weight,
    feedforward_gain,
    gate_weight,
    up_weight,
    down_weight,
):
    tp_count = lax.axis_size("tp")
    seq_count = lax.axis_size("seq")
    row_count, share_rows, model_width = hidden_in.shape
    span_rows = share_rows * tp_count
    row_length = span_rows * seq_count
    key_heads = key_weight.shape[1] // HEAD
    group_size = query_weight.shape[1] // key_weight.shape[1]
    scale_by = HEAD ** (-0.5)
    segment, within = doc_tables(document_lengths, row_length)
    first_place = lax.axis_index("seq") * span_rows
    query_segment = lax.dynamic_slice_in_dim(segment, first_place, span_rows, 1)
    query_within = lax.dynamic_slice_in_dim(within, first_place, span_rows, 1)
    query_places = first_place + jnp.arange(span_rows, dtype=jnp.int32)
    key_places = jnp.arange(row_length, dtype=jnp.int32)
    allowed = (key_places[None, None, :] <= query_places[None, :, None]) & (
        segment[:, None, :] == query_segment[:, :, None]
    )
    cos_table, sin_table = rope_tables(query_within, HEAD)
    hidden_float = hidden_in.astype(jnp.float32)

    def front(hidden_base):
        norm1_share, norm1_inverse = rms_forward(hidden_base, attention_gain)
        normed1 = lax.all_gather(norm1_share.astype(jnp.bfloat16), "tp", axis=1, tiled=True)
        query_raw = project(normed1, query_weight).reshape(
            row_count, span_rows, key_heads * group_size, HEAD
        )
        key_raw = project(normed1, key_weight).reshape(row_count, span_rows, key_heads, HEAD)
        value_local = project(normed1, value_weight).astype(jnp.bfloat16)
        query_normed, query_inverse = rms_forward(query_raw, query_gain)
        key_normed, key_inverse = rms_forward(key_raw, key_gain)
        queries = rotate(query_normed, cos_table, sin_table).astype(jnp.bfloat16)
        queries = queries.reshape(row_count, span_rows, key_heads, group_size, HEAD)
        key_local = (
            rotate(key_normed, cos_table, sin_table)
            .astype(jnp.bfloat16)
            .reshape(row_count, span_rows, key_heads * HEAD)
        )
        all_keys, all_values = (
            lax.all_gather(key_local, "seq", axis=1, tiled=True),
            lax.all_gather(value_local, "seq", axis=1, tiled=True),
        )
        all_keys = all_keys.reshape(row_count, row_length, key_heads, HEAD)
        all_values = all_values.reshape(row_count, row_length, key_heads, HEAD)
        attended, log_sums = attend_forward(queries, all_keys, all_values, allowed, scale_by)
        attn_out = attended.reshape(row_count, span_rows, key_heads * group_size * HEAD).astype(
            jnp.bfloat16
        )
        attn_share = lax.psum_scatter(
            project(attn_out, output_weight).astype(jnp.bfloat16), "tp", scatter_dimension=1, tiled=True
        ).astype(jnp.float32)
        middle = hidden_base + attn_share
        norm2_share, norm2_inverse = rms_forward(middle, feedforward_gain)
        normed2 = lax.all_gather(norm2_share.astype(jnp.bfloat16), "tp", axis=1, tiled=True)
        gate_act = project(normed2, gate_weight)
        up_act = project(normed2, up_weight)
        hidden_mid = (jax.nn.silu(gate_act) * up_act).astype(jnp.bfloat16)
        return (
            norm1_inverse,
            normed1,
            query_raw,
            query_inverse,
            key_raw,
            key_inverse,
            queries,
            all_keys,
            all_values,
            log_sums,
            attn_out,
            middle,
            norm2_inverse,
            normed2,
            gate_act,
            up_act,
            hidden_mid,
        )

    state = front(hidden_float)
    feedforward_share = lax.psum_scatter(
        project(state[16], down_weight).astype(jnp.bfloat16), "tp", scatter_dimension=1, tiled=True
    ).astype(jnp.float32)
    block_out = (state[11] + feedforward_share).astype(jnp.bfloat16)
    (
        norm1_inverse,
        normed1,
        query_raw,
        query_inverse,
        key_raw,
        key_inverse,
        queries,
        all_keys,
        all_values,
        log_sums,
        attn_out,
        middle,
        norm2_inverse,
        normed2,
        gate_act,
        up_act,
        hidden_mid,
    ) = state
    out_rows = lax.all_gather(output_grad, "tp", axis=1, tiled=True)
    mid_grad = jnp.einsum("rcd,fd->rcf", out_rows, down_weight, preferred_element_type=jnp.float32)
    down_grad = weight_grad(hidden_mid, out_rows)
    sigmoid_gate = jax.nn.sigmoid(gate_act)
    gate_grad = (mid_grad * up_act * sigmoid_gate * (1.0 + gate_act * (1.0 - sigmoid_gate))).astype(
        jnp.bfloat16
    )
    up_grad = (mid_grad * gate_act * sigmoid_gate).astype(jnp.bfloat16)
    gate_total = weight_grad(normed2, gate_grad)
    up_total = weight_grad(normed2, up_grad)
    normed2_part = project_back(gate_grad, gate_weight) + project_back(up_grad, up_weight)
    normed2_grad = lax.psum_scatter(
        normed2_part.astype(jnp.bfloat16), "tp", scatter_dimension=1, tiled=True
    ).astype(jnp.float32)
    middle_through, feedforward_gain_part = rms_backward(
        middle, norm2_inverse, feedforward_gain, normed2_grad
    )
    middle_grad = output_grad.astype(jnp.float32) + middle_through
    branch_grad = lax.all_gather(middle_grad.astype(jnp.bfloat16), "tp", axis=1, tiled=True)
    output_total = weight_grad(attn_out, branch_grad)
    attn_grad = project_back(branch_grad, output_weight).astype(jnp.bfloat16)
    attn_grad = attn_grad.reshape(row_count, span_rows, key_heads, group_size, HEAD)
    query_rot_grad, key_rot_all, value_grad_all = attend_backward(
        queries, all_keys, all_values, attn_grad, log_sums, allowed, scale_by
    )
    key_rot_grad, value_grad = (
        lax.psum_scatter(
            key_rot_all.reshape(row_count, row_length, key_heads * HEAD).astype(jnp.bfloat16),
            "seq",
            scatter_dimension=1,
            tiled=True,
        ).astype(jnp.float32),
        lax.psum_scatter(
            value_grad_all.reshape(row_count, row_length, key_heads * HEAD).astype(jnp.bfloat16),
            "seq",
            scatter_dimension=1,
            tiled=True,
        ).astype(jnp.float32),
    )
    query_unrot = unrotate(
        query_rot_grad.reshape(row_count, span_rows, key_heads * group_size, HEAD),
        cos_table,
        sin_table,
    )
    query_raw_grad, query_gain_part = rms_backward(
        query_raw, query_inverse, query_gain, query_unrot
    )
    key_unrot = unrotate(
        key_rot_grad.reshape(row_count, span_rows, key_heads, HEAD), cos_table, sin_table
    )
    key_raw_grad, key_gain_part = rms_backward(key_raw, key_inverse, key_gain, key_unrot)
    query_low = query_raw_grad.reshape(row_count, span_rows, key_heads * group_size * HEAD).astype(
        jnp.bfloat16
    )
    key_low = key_raw_grad.reshape(row_count, span_rows, key_heads * HEAD).astype(jnp.bfloat16)
    value_low = value_grad.astype(jnp.bfloat16)
    query_total = weight_grad(normed1, query_low)
    key_total = weight_grad(normed1, key_low)
    value_total = weight_grad(normed1, value_low)
    normed1_part = (
        project_back(query_low, query_weight)
        + project_back(key_low, key_weight)
        + project_back(value_low, value_weight)
    )
    normed1_grad = lax.psum_scatter(
        normed1_part.astype(jnp.bfloat16), "tp", scatter_dimension=1, tiled=True
    ).astype(jnp.float32)
    input_through, attention_gain_part = rms_backward(
        hidden_float, norm1_inverse, attention_gain, normed1_grad
    )
    input_grad = middle_grad + input_through
    attention_gain_grad, query_gain_grad, key_gain_grad, feedforward_gain_grad = lax.psum(
        (attention_gain_part, query_gain_part, key_gain_part, feedforward_gain_part), ("seq", "tp")
    )
    query_total, key_total, value_total, output_total, gate_total, up_total, down_grad = (
        lax.psum(query_total.astype(jnp.bfloat16), "seq").astype(jnp.float32),
        lax.psum(key_total.astype(jnp.bfloat16), "seq").astype(jnp.float32),
        lax.psum(value_total.astype(jnp.bfloat16), "seq").astype(jnp.float32),
        lax.psum(output_total.astype(jnp.bfloat16), "seq").astype(jnp.float32),
        lax.psum(gate_total.astype(jnp.bfloat16), "seq").astype(jnp.float32),
        lax.psum(up_total.astype(jnp.bfloat16), "seq").astype(jnp.float32),
        lax.psum(down_grad.astype(jnp.bfloat16), "seq").astype(jnp.float32),
    )
    return (
        block_out,
        input_grad,
        attention_gain_grad,
        query_total,
        key_total,
        value_total,
        query_gain_grad,
        key_gain_grad,
        output_total,
        feedforward_gain_grad,
        gate_total,
        up_total,
        down_grad,
    )


def solution(mesh):
    in_specs = (
        P(None, ("seq", "tp"), None),
        P(None, ("seq", "tp"), None),
        P(),
        P(),
        P(None, "tp"),
        P(None, "tp"),
        P(None, "tp"),
        P(),
        P(),
        P("tp", None),
        P(),
        P(None, "tp"),
        P(None, "tp"),
        P("tp", None),
    )
    out_specs = (
        P(None, ("seq", "tp"), None),
        P(None, ("seq", "tp"), None),
        P(),
        P(None, "tp"),
        P(None, "tp"),
        P(None, "tp"),
        P(),
        P(),
        P("tp", None),
        P(),
        P(None, "tp"),
        P(None, "tp"),
        P("tp", None),
    )
    return jax.shard_map(body, mesh=mesh, in_specs=in_specs, out_specs=out_specs, check_vma=False)
```

```python
import functools
import math

import jax
import jax.numpy as jnp
from jax import lax
from jax.experimental import pallas as pl
from jax.experimental.pallas import tpu as pltpu
from jax.sharding import PartitionSpec as P

HEAD = 128
EPS = 1e-06
ROPE_BASE = 1000000.0
MASKED = -1e30
LOG2E = math.log2(math.e)
BF = jnp.bfloat16
F32 = jnp.float32
I32 = jnp.int32


def sds(shape, dtype):
    return jax.ShapeDtypeStruct(shape, dtype)


def hbm(shape, dtype):
    return pltpu.HBM(shape, dtype)


def whole(shape):
    return pl.BlockSpec(shape, lambda *_: (0,) * len(shape))


def dot_nn(a, b):
    return lax.dot_general(a, b, (((1,), (0,)), ((), ())), preferred_element_type=F32)


def dot_nt(a, b):
    return lax.dot_general(a, b, (((1,), (1,)), ((), ())), preferred_element_type=F32)


def dot_tn(a, b):
    return lax.dot_general(a, b, (((0,), (0,)), ((), ())), preferred_element_type=F32)


def in_hbm(value):
    return pltpu.with_memory_space_constraint(value, pltpu.HBM)


def call(body, grid, in_specs, out_specs, out_shape, scratch, operands, mib, prefetch=1, after=(), aliases={}):
    after = (*ORDER, *after)
    at, extra = prefetch + len(in_specs), len(after)

    def run(*refs):
        return body(*refs[:at], *refs[at + extra :])

    operands = operands[:prefetch] + tuple(in_hbm(v) for v in operands[prefetch:])
    outs = pl.pallas_call(
        run,
        grid_spec=pltpu.PrefetchScalarGridSpec(
            num_scalar_prefetch=prefetch,
            grid=grid,
            in_specs=in_specs + [pl.BlockSpec(memory_space=pl.ANY)] * extra,
            out_specs=out_specs,
            scratch_shapes=scratch,
        ),
        out_shape=out_shape,
        input_output_aliases=aliases,
        compiler_params=pltpu.CompilerParams(
            vmem_limit_bytes=mib << 20, dimension_semantics=("arbitrary",) * len(grid)
        ),
        cost_estimate=pl.CostEstimate(flops=1, bytes_accessed=1, transcendentals=0),
    )(*operands, *(in_hbm(v) for v in after))
    ORDER[:] = [outs[0]]
    return outs


ORDER = []


def flip(axis, mask):
    return [(i, i ^ mask) for i in range(lax.axis_size(axis))]


def swap(value, axis, mask):
    return lax.ppermute(value, axis, flip(axis, mask))


def gather_tp(share):
    rows, _, width = share.shape
    return lax.all_gather(share, "tp", axis=1, tiled=True).reshape(-1, width)


def scatter_tp(part, row_count):
    part = part.reshape(row_count, -1, part.shape[1])
    return lax.psum_scatter(part, "tp", scatter_dimension=1, tiled=True)


def half_out(x_ref, core, keep_ref, send_ref):
    half = keep_ref.shape[1]
    keep_ref[...] = x_ref[:, pl.ds(pl.multiple_of(core * half, half), half)]
    send_ref[...] = x_ref[:, pl.ds(pl.multiple_of((1 - core) * half, half), half)]


def qkv_kernel(row_count, meta, x, wq, wk, wv, gq, gk, cos, sin, q_out, kv_out, q_raw, k_raw, keep, send, acc_q, acc_k, acc_v):
    j, last = pl.program_id(0), pl.num_programs(0) - 1

    @pl.when(j == 0)
    def _():
        half_out(x, meta[0], keep, send)
        acc_q[...] = jnp.zeros_like(acc_q)
        acc_k[...] = jnp.zeros_like(acc_k)
        acc_v[...] = jnp.zeros_like(acc_v)

    depth = wq.shape[0]
    xs = x[:, pl.ds(pl.multiple_of(j * depth, depth), depth)]
    acc_q[...] += dot_nn(xs, wq[...])
    acc_k[...] += dot_nn(xs, wk[...])
    acc_v[...] += dot_nn(xs, wv[...])

    @pl.when(j == last)
    def _():
        def turn(raw, gain):
            inverse = lax.rsqrt(jnp.mean(raw * raw, axis=-1, keepdims=True) + EPS)
            normed = raw * inverse * gain
            return (normed * cos[...] + pltpu.roll(normed, HEAD // 2, 1) * sin[...]).astype(BF)

        q_raw[...] = acc_q[...]
        k_raw[...] = acc_k[...]
        for h in range(acc_q.shape[1] // HEAD):
            at = slice(h * HEAD, (h + 1) * HEAD)
            q_out[:, at] = turn(acc_q[:, at], gq[...])
        span = kv_out.shape[2]
        for h in range(acc_k.shape[1] // HEAD):
            at = slice(h * HEAD, (h + 1) * HEAD)
            turned = turn(acc_k[:, at], gk[...])
            for r in range(row_count):
                kv_out[r, 0, :, at] = turned[r * span : (r + 1) * span]
        for r in range(row_count):
            kv_out[r, 1] = acc_v[r * span : (r + 1) * span, :].astype(BF)


def qkv_call(meta, row_count, x, weights, gains, tables):
    tokens, width = x.shape
    nq, nk = weights[0].shape[1], weights[1].shape[1]
    depth = width // 4
    row = lambda n: pl.BlockSpec((depth, n), lambda j, *_: (j, 0))
    kv = (row_count, 2, tokens // row_count, nk)
    return call(
        functools.partial(qkv_kernel, row_count),
        (4,),
        [whole((tokens, width)), row(nq), row(nk), row(nk)]
        + [whole((1, HEAD))] * 2
        + [whole((tokens, HEAD))] * 2,
        [whole((tokens, nq)), whole(kv), whole((tokens, nq)), whole((tokens, nk))]
        + [whole((tokens, width // 2))] * 2,
        [hbm((tokens, nq), BF), hbm(kv, BF), hbm((tokens, nq), F32), hbm((tokens, nk), F32)]
        + [hbm((tokens, width // 2), BF)] * 2,
        [pltpu.VMEM((tokens, nq), F32), pltpu.VMEM((tokens, nk), F32), pltpu.VMEM((tokens, nk), F32)],
        (meta, x, *weights, *gains, *tables),
        40,
    )


def stack_heads(ref, group):
    return jnp.concatenate([ref[:, h * HEAD : (h + 1) * HEAD] for h in range(group)], axis=0)


def tall(ref, group):
    return jnp.concatenate([ref[...]] * group, axis=0)


def attend_kernel(slot_count, group, scale, meta, *refs):
    q_ref, refs = refs[0], refs[1:]
    keys, refs = refs[:slot_count], refs[slot_count:]
    q_place, q_start, k_place, wo = refs[:4]
    o_out, lse_out, part_out = refs[4:7]
    scores, acc = refs[7:]
    r, g, last = pl.program_id(0), pl.program_id(1), pl.num_programs(1) - 1
    first = r * slot_count
    bases = pl.num_programs(0) * slot_count
    span = q_ref.shape[0]
    queries = stack_heads(q_ref, group)
    low = tall(q_start, group)
    high = tall(q_place, group)
    top = jnp.full((group * span, HEAD), MASKED, F32)

    for s in range(slot_count):

        def some(top, s=s):
            raw = dot_nt(queries, keys[s][0, 0]) * scale
            place = k_place[...] + meta[bases + s]
            kept = jnp.where((place >= low) & (place <= high), raw, MASKED)
            scores[s] = kept
            for c in range(span // HEAD):
                top = jnp.maximum(top, kept[:, c * HEAD : (c + 1) * HEAD])
            return top

        top = lax.cond(meta[first + s] > 0, some, lambda t: t, top)

    peak = jnp.max(top, axis=-1, keepdims=True)
    total = jnp.zeros((group * span, HEAD), F32)
    out = jnp.zeros((group * span, HEAD), F32)
    for s in range(slot_count):

        def more(carry, s=s):
            total, out = carry
            power = jnp.exp2(scores[s] - peak)
            for c in range(span // HEAD):
                total = total + power[:, c * HEAD : (c + 1) * HEAD]
            return total, out + dot_nn(power.astype(BF), keys[s][0, 1])

        total, out = lax.cond(meta[first + s] > 0, more, lambda t: t, (total, out))

    total = jnp.sum(total, axis=-1, keepdims=True)
    lse_out[0, 0] = peak + jnp.log2(total)
    out = (out / total).astype(BF)
    out = jnp.concatenate([out[h * span : (h + 1) * span] for h in range(group)], axis=1)
    o_out[...] = out
    part = dot_nn(out, wo[...])

    @pl.when(g == 0)
    def _():
        acc[...] = part

    @pl.when(g > 0)
    def _():
        acc[...] += part

    @pl.when(g == last)
    def _():
        part_out[...] = acc[...].astype(BF)


def attend_call(meta, queries, kv_slots, places, wo):
    slot_count = len(kv_slots)
    tokens, nq = queries.shape
    row_count, _, span, nk = kv_slots[0].shape
    heads, group = nk // HEAD, nq // nk
    width = wo.shape[1]
    wide = group * HEAD
    rows = pl.BlockSpec((span, wide), lambda r, g, *_: (r, g))
    column = pl.BlockSpec((span, 1), lambda r, g, *_: (r, 0))
    return call(
        functools.partial(attend_kernel, slot_count, group, HEAD**-0.5 * LOG2E),
        (row_count, heads),
        [rows]
        + [pl.BlockSpec((1, 2, span, HEAD), lambda r, g, *_: (r, 0, 0, g))] * slot_count
        + [column, column, whole((1, span))]
        + [pl.BlockSpec((wide, width), lambda r, g, *_: (g, 0))],
        [
            rows,
            pl.BlockSpec((1, 1, group * span, 1), lambda r, g, *_: (r, g, 0, 0)),
            pl.BlockSpec((span, width), lambda r, g, *_: (r, 0)),
        ],
        [hbm((tokens, nq), BF), hbm((row_count, heads, group * span, 1), F32), hbm((tokens, width), BF)],
        [pltpu.VMEM((slot_count, group * span, span), F32), pltpu.VMEM((span, width), F32)],
        (meta, queries, *kv_slots, *places, wo),
        40,
    )


def ff_kernel(meta, x, og, wg, wu, wd, hm_out, gu_out, grad_out, keep, send, acc):
    j, last = pl.program_id(0), pl.num_programs(0) - 1

    @pl.when(j == 0)
    def _():
        half_out(x, meta[0], keep, send)
        acc[...] = jnp.zeros_like(acc)

    gate = dot_nn(x[...], wg[...])
    up = dot_nn(x[...], wu[...])
    upstream = dot_nt(og[...], wd[...])
    sigmoid = 1.0 / (1.0 + jnp.exp(-gate))
    silu = gate * sigmoid
    gate_grad = (upstream * up * sigmoid * (1.0 + gate * (1.0 - sigmoid))).astype(BF)
    up_grad = (upstream * silu).astype(BF)
    hm_out[...] = (silu * up).astype(BF)
    gu_out[0] = gate_grad
    gu_out[1] = up_grad
    acc[...] += dot_nt(gate_grad, wg[...]) + dot_nt(up_grad, wu[...])

    @pl.when(j == last)
    def _():
        grad_out[...] = acc[...].astype(BF)


def ff_call(meta, x, og, wg, wu, wd, after):
    tokens, width = x.shape
    hidden = wg.shape[1]
    block = 256
    column = pl.BlockSpec((width, block), lambda j, *_: (0, j))
    return call(
        ff_kernel,
        (hidden // block,),
        [whole((tokens, width))] * 2 + [column, column, pl.BlockSpec((block, width), lambda j, *_: (j, 0))],
        [
            pl.BlockSpec((tokens, block), lambda j, *_: (0, j)),
            pl.BlockSpec((2, tokens, block), lambda j, *_: (0, 0, j)),
            whole((tokens, width)),
            whole((tokens, width // 2)),
            whole((tokens, width // 2)),
        ],
        [hbm((tokens, hidden), BF), hbm((2, tokens, hidden), BF), hbm((tokens, width), BF)]
        + [hbm((tokens, width // 2), BF)] * 2,
        [pltpu.VMEM((tokens, width), F32)],
        (meta, x, og, wg, wu, wd),
        48,
        after=after,
    )


def ff_out_kernel(hm, wd, out, acc):
    j, last = pl.program_id(0), pl.num_programs(0) - 1
    part = dot_nn(hm[...], wd[...])

    @pl.when(j == 0)
    def _():
        acc[...] = part

    @pl.when(j > 0)
    def _():
        acc[...] += part

    @pl.when(j == last)
    def _():
        out[...] = acc[...].astype(BF)


def ff_out_call(hm, wd):
    tokens, hidden = hm.shape
    width = wd.shape[1]
    block = hidden // 3
    return call(
        ff_out_kernel,
        (3,),
        [pl.BlockSpec((tokens, block), lambda j: (0, j)), pl.BlockSpec((block, width), lambda j: (j, 0))],
        [whole((tokens, width))],
        [hbm((tokens, width), BF)],
        [pltpu.VMEM((tokens, width), F32)],
        (hm, wd),
        32,
        prefetch=0,
    )[0]


def norm_back(turned, raw, gain, cos, sin):
    upstream = turned * cos - pltpu.roll(turned, HEAD // 2, 1) * sin
    inverse = lax.rsqrt(jnp.mean(raw * raw, axis=-1, keepdims=True) + EPS)
    scaled = upstream * gain
    through = inverse * scaled - raw * (inverse * inverse * inverse) * jnp.mean(
        raw * scaled, axis=-1, keepdims=True
    )
    return through.astype(BF), jnp.sum(upstream * raw * inverse, axis=0, keepdims=True)


def attend_back_kernel(slot_count, group, scale, meta, *refs):
    bg, wo, q_ref, refs = refs[0], refs[1], refs[2], refs[3:]
    keys, refs = refs[:slot_count], refs[slot_count:]
    o_ref, lse_ref, q_place, q_start, k_place, q_raw, gq, cos, sin = refs[:9]
    dq_out, even_out, odd_out, gain_out, keep, send = refs[9:15]
    r, g = pl.program_id(0), pl.program_id(1)
    first = r * slot_count
    bases = pl.num_programs(0) * slot_count

    @pl.when(g == 0)
    def _():
        half_out(bg, meta[bases + slot_count], keep, send)

    @pl.when((r == 0) & (g == 0))
    def _():
        gain_out[...] = jnp.zeros_like(gain_out)

    span = q_ref.shape[0]
    d_out = dot_nt(bg[...], wo[...]).astype(BF)
    d_out = jnp.concatenate([d_out[:, h * HEAD : (h + 1) * HEAD] for h in range(group)], axis=0)
    o_rows = stack_heads(o_ref, group)
    queries = stack_heads(q_ref, group)
    centre = jnp.sum(d_out.astype(F32) * o_rows.astype(F32), axis=-1, keepdims=True)
    lse = lse_ref[0, 0]
    low = tall(q_start, group)
    high = tall(q_place, group)
    dq = jnp.zeros((group * span, HEAD), F32)
    for s in range(slot_count):
        out = (odd_out if s % 2 else even_out).at[s // 2, 0]

        def some(dq, s=s, out=out):
            raw = dot_nt(queries, keys[s][0, 0]) * (scale * LOG2E)
            place = k_place[...] + meta[bases + s]
            probs = jnp.where((place >= low) & (place <= high), jnp.exp2(raw - lse), 0.0)
            d_probs = dot_nt(d_out, keys[s][0, 1])
            d_score = (probs * (d_probs - centre)).astype(BF)
            out[0] = (dot_tn(d_score, queries) * scale).astype(BF)
            out[1] = dot_tn(probs.astype(BF), d_out).astype(BF)
            return dq + dot_nn(d_score, keys[s][0, 0])

        def none(dq, out=out):
            out[...] = jnp.zeros(out.shape, BF)
            return dq

        dq = lax.cond(meta[first + s] > 0, some, none, dq)

    gain = gq[...]
    gain_total = jnp.zeros((1, HEAD), F32)
    for h in range(group):
        rows = dq[h * span : (h + 1) * span] * scale
        d_raw, part = norm_back(rows, q_raw[:, h * HEAD : (h + 1) * HEAD], gain, cos[...], sin[...])
        dq_out[:, h * HEAD : (h + 1) * HEAD] = d_raw
        gain_total = gain_total + part
    gain_out[...] += gain_total


def attend_back_call(meta, bg, wo, queries, kv_slots, attended, lse, places, q_raw, gq, tables):
    slot_count = len(kv_slots)
    tokens, width = bg.shape
    nq = queries.shape[1]
    row_count, _, span, nk = kv_slots[0].shape
    heads, group = nk // HEAD, nq // nk
    wide = group * HEAD
    rows = pl.BlockSpec((span, wide), lambda r, g, *_: (r, g))
    by_row = lambda n: pl.BlockSpec((span, n), lambda r, g, *_: (r, 0))
    kv_out = pl.BlockSpec((slot_count // 2, 1, 2, span, HEAD), lambda r, g, *_: (0, r, 0, 0, g))
    kv_shape = (slot_count // 2, row_count, 2, span, nk)
    return call(
        functools.partial(attend_back_kernel, slot_count, group, HEAD**-0.5),
        (row_count, heads),
        [by_row(width), pl.BlockSpec((wide, width), lambda r, g, *_: (g, 0)), rows]
        + [pl.BlockSpec((1, 2, span, HEAD), lambda r, g, *_: (r, 0, 0, g))] * slot_count
        + [rows, pl.BlockSpec((1, 1, group * span, 1), lambda r, g, *_: (r, g, 0, 0))]
        + [by_row(1), by_row(1), whole((1, span))]
        + [rows, whole((1, HEAD)), by_row(HEAD), by_row(HEAD)],
        [rows, kv_out, kv_out, whole((1, HEAD)), by_row(width // 2), by_row(width // 2)],
        [
            hbm((tokens, nq), BF),
            hbm(kv_shape, BF),
            hbm(kv_shape, BF),
            sds((1, HEAD), F32),
            hbm((tokens, width // 2), BF),
            hbm((tokens, width // 2), BF),
        ],
        [],
        (meta, bg, wo, queries, *kv_slots, attended, lse, *places, q_raw, gq, *tables),
        40,
    )


def back_kernel(count, row_count, *refs):
    pieces, refs = refs[:count], refs[count:]
    dq_ref, k_raw, gk, cos, sin, wq, wk, wv = refs[:8]
    all_out, part_out, gain_out = refs[8:11]
    j = pl.program_id(0)
    nq, nk = wq.shape[1], wk.shape[1]
    span = pieces[0].shape[2]

    @pl.when(j == 0)
    def _():
        all_out[:, :nq] = dq_ref[...]
        gain_total = jnp.zeros((1, HEAD), F32)
        for r in range(row_count):
            rows = slice(r * span, (r + 1) * span)
            for h in range(nk // HEAD):
                at = slice(h * HEAD, (h + 1) * HEAD)
                turned = sum(p[r, 0, :, at].astype(F32) for p in pieces)
                d_raw, part = norm_back(turned, k_raw[rows, at], gk[...], cos[rows], sin[rows])
                all_out[rows, nq + h * HEAD : nq + (h + 1) * HEAD] = d_raw
                gain_total = gain_total + part
            all_out[rows, nq + nk :] = sum(p[r, 1].astype(F32) for p in pieces).astype(BF)
        gain_out[...] = gain_total

    part = (
        dot_nt(all_out[:, :nq], wq[...])
        + dot_nt(all_out[:, nq : nq + nk], wk[...])
        + dot_nt(all_out[:, nq + nk :], wv[...])
    )
    part_out[...] = part.astype(BF)


def back_call(pieces, dq, k_raw, gk, tables, weights):
    tokens, nq = dq.shape
    nk = k_raw.shape[1]
    width = weights[0].shape[0]
    block = width // 4
    row = lambda n: pl.BlockSpec((block, n), lambda j, *_: (j, 0))
    return call(
        functools.partial(back_kernel, len(pieces), pieces[0].shape[0]),
        (4,),
        [whole(pieces[0].shape)] * len(pieces)
        + [whole((tokens, nq)), whole((tokens, nk)), whole((1, HEAD)), whole((tokens, HEAD)), whole((tokens, HEAD))]
        + [row(nq), row(nk), row(nk)],
        [whole((tokens, nq + 2 * nk)), pl.BlockSpec((tokens, block), lambda j, *_: (0, j)), whole((1, HEAD))],
        [hbm((tokens, nq + 2 * nk), BF), hbm((tokens, width), BF), sds((1, HEAD), F32)],
        [],
        (*pieces, dq, k_raw, gk, *tables, *weights),
        40,
        prefetch=0,
    )


def grad_kernel(count, ids, *refs):
    lefts, rights = refs[:count], refs[count : 2 * count]
    a_out, b_out = refs[2 * count :]
    f = pl.program_id(1)

    def put(out):
        if len(out.shape) == 3:
            for n in range(out.shape[0]):
                out[n] = sum(dot_tn(x[...], r[n]) for x, r in zip(lefts, rights)).astype(BF)
        else:
            out[...] = sum(dot_tn(x[...], r[...]) for x, r in zip(lefts, rights)).astype(BF)

    @pl.when(f == 0)
    def _():
        put(a_out)

    @pl.when(f == 1)
    def _():
        put(b_out)


def grad_call(ids, rows, lefts, rights):
    tokens, cols = rights[0].shape[-2:]
    lead = rights[0].shape[:-2]
    zeros = (0,) * len(lead)
    n = math.prod(lead) * cols
    wide = next(w for w in (512, 384, 256, 128) if cols % w == 0)
    out_a = pl.BlockSpec((*lead, rows, wide), lambda c, f, ids: (*zeros, 0, c))
    out_b = pl.BlockSpec((*lead, rows, wide), lambda c, f, ids: (*zeros, 0, jnp.where(f == 0, jnp.maximum(c - 1, 0), c)))
    return call(
        functools.partial(grad_kernel, len(lefts)),
        (cols // wide, 2),
        [pl.BlockSpec((tokens, rows), lambda c, f, ids: (0, ids[f]))] * len(lefts)
        + [pl.BlockSpec((*lead, tokens, wide), lambda c, f, ids: (*zeros, 0, c))] * len(rights),
        [out_a, out_b],
        [hbm((*lead, rows, cols), BF)] * 2,
        [],
        (ids, *lefts, *rights),
        40,
    )


def split_kernel(bits, keep_a, got_a, keep_b, got_b, send_a, next_a, send_b, next_b):
    j = pl.program_id(0)

    def put(out, keep, got):
        out[...] = (keep[...].astype(F32) + got[...].astype(F32)).astype(BF)

    @pl.when(j == 0)
    def _():
        put(send_a, keep_a, got_a)
        put(send_b, keep_b, got_b)

    @pl.when(j == 1)
    def _():
        put(next_a, keep_a, got_a)
        put(next_b, keep_b, got_b)


def split_call(bits, keeps, gots):
    *lead, rows, cols = keeps[0].shape
    zeros = (0,) * len(lead)
    half = (*lead, rows // 2, cols)
    part = lambda f: pl.BlockSpec(half, lambda j, bits: (*zeros, jnp.where(j == 0, 1 - bits[f], bits[f]), 0))
    send_a, next_a, send_b, next_b = call(
        split_kernel,
        (2,),
        [part(0), part(0), part(1), part(1)],
        [whole(half)] * 4,
        [hbm(half, BF)] * 4,
        [],
        (bits, keeps[0], gots[0], keeps[1], gots[1]),
        40,
    )
    return (send_a, send_b), (next_a, next_b)


def add_kernel(keep_a, got_a, keep_b, got_b, out_a, out_b):
    out_a[...] = (keep_a[...].astype(F32) + got_a[...].astype(F32)).astype(BF)
    out_b[...] = (keep_b[...].astype(F32) + got_b[...].astype(F32)).astype(BF)


def add_call(keeps, gots):
    shape = keeps[0].shape
    return call(
        add_kernel,
        (1,),
        [whole(shape)] * 4,
        [whole(shape)] * 2,
        [hbm(shape, BF)] * 2,
        [],
        (keeps[0], gots[0], keeps[1], gots[1]),
        40,
        prefetch=0,
    )


def put_wide(piece, outs, split):
    if len(piece.shape) == 3:
        for n, out in enumerate(outs):
            out[...] = piece[n].astype(F32)
    else:
        at = 0
        for out, wide in zip(outs, split):
            out[...] = piece[:, at : at + wide].astype(F32)
            at += wide


def widen_kernel(count, split, table, *refs):
    pieces, joined, outs = refs[:count], refs[count], refs[count + 1 :]
    j = pl.program_id(0)
    for k, ref in enumerate(pieces):

        @pl.when(j == k)
        def _(ref=ref):
            joined[...] = ref[...]
            put_wide(ref, outs, split)


def widen_split(pieces, shapes, by_rows):
    lead, cols = pieces[0].shape[:-2], pieces[0].shape[-1]
    split = [cols] if not by_rows or lead else [s[1] for s in shapes]
    return split * len(shapes) if lead else split


def widen_call(table, pieces, shapes, by_rows):
    *lead, rows, cols = pieces[0].shape
    zeros = (0,) * len(lead)
    split = widen_split(pieces, shapes, by_rows)
    count = len(pieces)
    return call(
        functools.partial(widen_kernel, count, split),
        (count,),
        [whole(pieces[0].shape)] * count,
        [pl.BlockSpec((*lead, rows, cols), lambda j, t: (*zeros, j, 0))]
        + [pl.BlockSpec((rows, w), lambda j, t: (t[0, j], t[1, j])) for w in split],
        [hbm((*lead, count * rows, cols), BF)] + [hbm(s, F32) for s in shapes],
        [],
        (table, *pieces),
        48,
    )


def widen_other_kernel(count, split, table, joined, *refs):
    put_wide(joined, refs[count:], split)


def widen_other_call(table, joined, outs, by_rows):
    *lead, rows, cols = joined.shape
    zeros = (0,) * len(lead)
    count = table.shape[1]
    shapes = [o.shape for o in outs]
    split = widen_split([joined], shapes, by_rows)
    return call(
        functools.partial(widen_other_kernel, len(outs), split),
        (count,),
        [pl.BlockSpec((*lead, rows // count, cols), lambda j, t: (*zeros, j, 0))]
        + [pl.BlockSpec(memory_space=pl.ANY)] * len(outs),
        [pl.BlockSpec((rows // count, w), lambda j, t: (t[0, j], t[1, j])) for w in split],
        [hbm(s, F32) for s in shapes],
        [],
        (table, joined, *outs),
        40,
        aliases={2 + k: k for k in range(len(outs))},
    )


def norm_kernel(x, gain, out):
    value = x[...].astype(F32)
    inverse = lax.rsqrt(jnp.mean(value * value, axis=-1, keepdims=True) + EPS)
    out[...] = (value * inverse * gain[...]).astype(BF)


def norm_call(x, gain):
    return call(
        norm_kernel,
        (1,),
        [whole(x.shape), whole(gain.shape)],
        [whole(x.shape)],
        [hbm(x.shape, BF)],
        [],
        (x, gain),
        24,
        prefetch=0,
    )[0]


def middle_kernel(x, got, gain, middle, out):
    value = x[...].astype(F32) + got[...].astype(F32)
    inverse = lax.rsqrt(jnp.mean(value * value, axis=-1, keepdims=True) + EPS)
    middle[...] = value
    out[...] = (value * inverse * gain[...]).astype(BF)


def middle_call(x, got, gain, after):
    return call(
        middle_kernel,
        (1,),
        [whole(x.shape), whole(x.shape), whole(gain.shape)],
        [whole(x.shape)] * 2,
        [hbm(x.shape, F32), hbm(x.shape, BF)],
        [],
        (x, got, gain),
        24,
        prefetch=0,
        after=after,
    )


def norm_grad_kernel(x, got, base, gain, *outs):
    value, upstream = x[...].astype(F32), got[...].astype(F32)
    inverse = lax.rsqrt(jnp.mean(value * value, axis=-1, keepdims=True) + EPS)
    scaled = upstream * gain[...]
    through = inverse * scaled - value * (inverse * inverse * inverse) * jnp.mean(
        value * scaled, axis=-1, keepdims=True
    )
    total = base[...].astype(F32) + through
    outs[0][...] = total
    outs[1][...] = jnp.sum(upstream * value * inverse, axis=0, keepdims=True)
    if len(outs) > 2:
        outs[2][...] = total.astype(BF)


def norm_grad_call(x, got, base, gain, low):
    return call(
        norm_grad_kernel,
        (1,),
        [whole(x.shape)] * 3 + [whole(gain.shape)],
        [whole(x.shape), whole(gain.shape)] + [whole(x.shape)] * low,
        [hbm(x.shape, F32), hbm(gain.shape, F32)] + [hbm(x.shape, BF)] * low,
        [],
        (x, got, base, gain),
        24,
        prefetch=0,
    )


def copy_kernel(x, out):
    out[...] = x[...]


def copy_call(x):
    return call(copy_kernel, (1,), [whole(x.shape)], [whole(x.shape)], [hbm(x.shape, x.dtype)], [], (x,), 24, prefetch=0)[0]


def flow_table(masks):
    seq = lax.axis_index("seq")
    slot = jnp.arange(1 << len(masks), dtype=I32)
    block = jnp.zeros_like(slot)
    for level, mask in enumerate(masks):
        shift = len(masks) - 1 - level
        block = block + (((seq & mask) // mask) ^ ((slot >> shift) & 1)) * (1 << shift)
    return block


class WeightSum:
    def __init__(self, lefts, rights, masks, shapes, by_rows):
        self.lefts, self.rights, self.shapes, self.by_rows = lefts, rights, shapes, by_rows
        self.flows = (masks, masks[::-1])
        seq = lax.axis_index("seq")
        core = seq & 1
        self.bits = [jnp.stack([(seq & m[k]) // m[k] for m in self.flows]) for k in range(len(masks))]
        self.level = 0
        slots = 1 << len(masks)
        inner = [flow_table(m) for m in self.flows]
        rows_of = jnp.concatenate([inner[0], slots + inner[1]])
        zero = jnp.zeros_like(rows_of)
        if by_rows:
            self.tables = [jnp.stack([half * 2 * slots + rows_of, zero]) for half in (core, 1 - core)]
        else:
            self.tables = [jnp.stack([rows_of, zero + half]) for half in (core, 1 - core)]

    def swap_level(self, sends):
        self.gots = [swap(s, "seq", m[self.level]) for s, m in zip(sends, self.flows)]
        self.level += 1

    def send(self):
        rows = self.lefts[0].shape[1]
        self.direct = rows % (4 * HEAD) == 0
        if self.direct:
            base = jnp.array([0, 2], I32)
            self.swap_level(grad_call(base + 1 - self.bits[0], rows // 4, self.lefts, self.rights))
        return self

    def keep(self):
        rows = self.lefts[0].shape[1]
        if self.direct:
            base = jnp.array([0, 2], I32)
            self.kept = grad_call(base + self.bits[0], rows // 4, self.lefts, self.rights)
        else:
            self.kept = grad_call(jnp.arange(2, dtype=I32), rows // 2, self.lefts, self.rights)
            half, at = rows // 4, self.kept[0].ndim - 2
            cut = lambda v, b: lax.dynamic_slice_in_dim(v, b * half, half, at)
            self.swap_level([cut(v, 1 - self.bits[0][f]) for f, v in enumerate(self.kept)])
            self.kept = [cut(v, self.bits[0][f]) for f, v in enumerate(self.kept)]
        return self

    def middle(self):
        while self.level < len(self.flows[0]):
            sends, self.kept = split_call(self.bits[self.level], self.kept, self.gots)
            self.swap_level(sends)
        return self

    def last(self):
        self.pieces = []
        for piece, masks in zip(add_call(self.kept, self.gots), self.flows):
            pieces = [piece]
            for mask in reversed(masks):
                pieces = [v for p in pieces for v in (p, None)]
                pieces[1::2] = [swap(p, "seq", mask) for p in pieces[::2]]
            self.pieces.append(pieces)
        return self

    def own(self):
        joined, *self.outs = widen_call(self.tables[0], self.ordered(), self.shapes, self.by_rows)
        self.joined = swap(joined, "seq", 1)
        return self

    def ordered(self):
        found = []
        levels = len(self.flows[0])
        for pieces in self.pieces:
            back = lambda s: sum(((s >> k) & 1) << (levels - 1 - k) for k in range(levels))
            found += [pieces[back(s)] for s in range(len(pieces))]
        return found

    def other(self):
        return widen_other_call(self.tables[1], self.joined, self.outs, self.by_rows)


def halves(value, core):
    half = value.shape[1] // 2
    return (
        lax.dynamic_slice_in_dim(value, core * half, half, 1),
        lax.dynamic_slice_in_dim(value, (1 - core) * half, half, 1),
    )


def body(
    hidden_in,
    output_grad,
    document_lengths,
    attention_gain,
    query_weight,
    key_weight,
    value_weight,
    query_gain,
    key_gain,
    output_weight,
    feedforward_gain,
    gate_weight,
    up_weight,
    down_weight,
):
    ORDER.clear()
    tp, seqs = lax.axis_size("tp"), lax.axis_size("seq")
    seq_at = lax.axis_index("seq")
    core = seq_at & 1
    row_count, share, width = hidden_in.shape
    span = share * tp
    masks = tuple(1 << b for b in range(1, seqs.bit_length() - 1))

    ends = jnp.stack(
        [jnp.sum(document_lengths[:, : n + 1], axis=1) for n in range(document_lengths.shape[1])], axis=1
    )
    starts = ends - document_lengths
    local = jnp.arange(span, dtype=I32)
    places = seq_at * span + local
    inside = (places[None, :, None] >= starts[:, None]) & (places[None, :, None] < ends[:, None])
    begun = jnp.sum(jnp.where(inside, starts[:, None], 0), axis=2)
    slot_seq = jnp.arange(seqs, dtype=I32) ^ seq_at
    needed = (slot_seq <= seq_at)[None] & ((slot_seq + 1)[None] * span > begun[:, :1])
    meta = jnp.concatenate([needed.astype(I32).reshape(-1), slot_seq * span, core[None]])
    place_set = (jnp.tile(places, row_count)[:, None], begun.reshape(-1, 1), local[None, :])
    frequency = ROPE_BASE ** (-2.0 * jnp.arange(HEAD // 2, dtype=F32) / HEAD)
    angles = (places[None] - begun).reshape(-1, 1).astype(F32) * frequency
    cos, sin = jnp.cos(angles), jnp.sin(angles)
    tables = (jnp.concatenate([cos, cos], 1), jnp.concatenate([-sin, sin], 1))
    core_meta = core[None]
    q_gain, k_gain = query_gain[None], key_gain[None]
    qkv_weights = (query_weight, key_weight, value_weight)

    flat = lambda v: v.reshape(-1, width)
    hidden, upward = flat(hidden_in), flat(output_grad)
    attn_gain, ff_gain = attention_gain[None], feedforward_gain[None]
    shares = lambda v: v.reshape(row_count, share, width)
    normed1 = gather_tp(shares(norm_call(hidden, attn_gain)))
    queries, kv, q_raw, k_raw, n1_keep, n1_send = qkv_call(
        core_meta, row_count, normed1, qkv_weights, (q_gain, k_gain), tables
    )
    grads = gather_tp(shares(copy_call(upward)))
    kv_slots = []
    for value in [kv] + [swap(kv, "seq", m) for m in range(2, seqs, 2)]:
        kv_slots += [value, swap(value, "seq", 1)]
    attended, lse, o_part = attend_call(meta, queries, kv_slots, place_set, output_weight)

    def both(own, sent=None):
        return [own, swap(own if sent is None else sent, "seq", 1)]

    o_both = both(attended)
    n1_both = both(n1_keep, n1_send)
    middle, normed2 = middle_call(hidden, flat(scatter_tp(o_part, row_count)), ff_gain, (grads,))
    grads_both = both(*halves(grads, core))
    normed2 = gather_tp(shares(normed2))
    hidden_mid, gate_up, n2_part, n2_keep, n2_send = ff_call(
        core_meta, normed2, grads, gate_weight, up_weight, down_weight, (grads_both[1], o_both[1], n1_both[1])
    )
    n2_got = scatter_tp(n2_part, row_count)

    down = WeightSum(both(hidden_mid), grads_both, masks, [down_weight.shape], False).send()
    gate = WeightSum(both(n2_keep, n2_send), both(gate_up), masks, [gate_weight.shape, up_weight.shape], True).send()
    down.keep()
    gate.keep()
    down.middle()
    middle_grad, ff_gain_grad, branch = norm_grad_call(middle, flat(n2_got), upward, ff_gain, True)
    branch = gather_tp(shares(branch))
    down.last()
    gate.middle()
    dq, even, odd, q_gain_grad, b_keep, b_send = attend_back_call(
        meta,
        branch,
        output_weight,
        queries,
        kv_slots,
        attended,
        lse,
        place_set,
        q_raw,
        q_gain,
        tables,
    )
    gate.last()
    odd = swap(odd, "seq", 1)
    chip = [(even[k].astype(F32) + odd[k].astype(F32)).astype(BF) for k in range(seqs // 2)]
    pieces = [chip[0]] + [swap(chip[m // 2], "seq", m) for m in range(2, seqs, 2)]
    out = WeightSum(o_both, both(b_keep, b_send), masks, [output_weight.shape], False).send().keep()
    ff_part = ff_out_call(hidden_mid, down_weight)
    ff_got = scatter_tp(ff_part, row_count)
    down.own()
    all_grad, n1_part, k_gain_grad = back_call(pieces, dq, k_raw, k_gain, tables, qkv_weights)
    n1_got = scatter_tp(n1_part, row_count)
    out.middle()
    qkv = WeightSum(n1_both, both(all_grad), masks, [w.shape for w in qkv_weights], True).send().keep()
    out.last()
    (down_out,) = down.other()
    qkv.middle()
    qkv.last()
    block_out = shares((middle + flat(ff_got).astype(F32)).astype(BF))
    input_grad, attn_gain_grad = norm_grad_call(hidden, flat(n1_got), middle_grad, attn_gain, False)
    input_grad = shares(input_grad)
    gate.own()
    out.own()
    gate_out, up_out = gate.other()
    (output_out,) = out.other()
    qkv.own()
    query_out, key_out, value_out = qkv.other()

    gains = jnp.concatenate(
        [v.reshape(-1) for v in (attn_gain_grad, ff_gain_grad, q_gain_grad, k_gain_grad)]
    ).reshape(-1, HEAD)
    for axis, size in (("tp", tp), ("seq", seqs)):
        mask = 1
        while mask < size:
            gains = gains + swap(gains, axis, mask)
            mask *= 2
    gains = gains.reshape(-1)
    return (
        block_out,
        input_grad,
        gains[:width],
        query_out,
        key_out,
        value_out,
        gains[2 * width : 2 * width + HEAD],
        gains[2 * width + HEAD :],
        output_out,
        gains[width : 2 * width],
        gate_out,
        up_out,
        down_out,
    )


def solution(mesh):
    tokens, columns, rows = P(None, ("seq", "tp"), None), P(None, "tp"), P("tp", None)
    in_specs = (
        tokens,
        tokens,
        P(),
        P(),
        columns,
        columns,
        columns,
        P(),
        P(),
        rows,
        P(),
        columns,
        columns,
        rows,
    )
    out_specs = (
        tokens,
        tokens,
        P(),
        columns,
        columns,
        columns,
        P(),
        P(),
        rows,
        P(),
        columns,
        columns,
        rows,
    )
    return jax.shard_map(body, mesh=mesh, in_specs=in_specs, out_specs=out_specs, check_vma=False)
```

```python
import functools
import math

import jax
import jax.numpy as jnp
from jax import lax
from jax.experimental import pallas as pl
from jax.experimental.pallas import tpu as pltpu
from jax.sharding import PartitionSpec as P

HEAD = 128
EPS = 1e-06
ROPE_BASE = 1000000.0
MASKED = -1e30
LOG2E = math.log2(math.e)
BF = jnp.bfloat16
F32 = jnp.float32
I32 = jnp.int32


def sds(shape, dtype):
    return jax.ShapeDtypeStruct(shape, dtype)


def hbm(shape, dtype):
    return pltpu.HBM(shape, dtype)


def whole(shape):
    return pl.BlockSpec(shape, lambda *_: (0,) * len(shape))


def dot_nn(a, b):
    return lax.dot_general(a, b, (((1,), (0,)), ((), ())), preferred_element_type=F32)


def dot_nt(a, b):
    return lax.dot_general(a, b, (((1,), (1,)), ((), ())), preferred_element_type=F32)


def dot_tn(a, b):
    return lax.dot_general(a, b, (((0,), (0,)), ((), ())), preferred_element_type=F32)


def in_hbm(value):
    return pltpu.with_memory_space_constraint(value, pltpu.HBM)


def call(body, grid, in_specs, out_specs, out_shape, scratch, operands, mib, prefetch=1, after=(), aliases={}):
    after = (*ORDER, *after)
    at, extra = prefetch + len(in_specs), len(after)

    def run(*refs):
        return body(*refs[:at], *refs[at + extra :])

    operands = operands[:prefetch] + tuple(in_hbm(v) for v in operands[prefetch:])
    outs = pl.pallas_call(
        run,
        grid_spec=pltpu.PrefetchScalarGridSpec(
            num_scalar_prefetch=prefetch,
            grid=grid,
            in_specs=in_specs + [pl.BlockSpec(memory_space=pl.ANY)] * extra,
            out_specs=out_specs,
            scratch_shapes=scratch,
        ),
        out_shape=out_shape,
        input_output_aliases=aliases,
        compiler_params=pltpu.CompilerParams(
            vmem_limit_bytes=mib << 20, dimension_semantics=("arbitrary",) * len(grid)
        ),
        cost_estimate=pl.CostEstimate(flops=1, bytes_accessed=1, transcendentals=0),
    )(*operands, *(in_hbm(v) for v in after))
    ORDER[:] = [outs[0]]
    return outs


ORDER = []


def flip(axis, mask):
    return [(i, i ^ mask) for i in range(lax.axis_size(axis))]


def swap(value, axis, mask):
    return lax.ppermute(value, axis, flip(axis, mask))


def gather_tp(share):
    rows, _, width = share.shape
    return lax.all_gather(share, "tp", axis=1, tiled=True).reshape(-1, width)


def scatter_tp(part, row_count):
    part = part.reshape(row_count, -1, part.shape[1])
    return lax.psum_scatter(part, "tp", scatter_dimension=1, tiled=True)


def half_out(x_ref, core, keep_ref, send_ref):
    half = keep_ref.shape[1]
    keep_ref[...] = x_ref[:, pl.ds(pl.multiple_of(core * half, half), half)]
    send_ref[...] = x_ref[:, pl.ds(pl.multiple_of((1 - core) * half, half), half)]


def qkv_kernel(row_count, meta, x, wq, wk, wv, gq, gk, cos, sin, q_out, kv_out, q_raw, k_raw, keep, send, acc_q, acc_k, acc_v):
    j, last = pl.program_id(0), pl.num_programs(0) - 1

    @pl.when(j == 0)
    def _():
        half_out(x, meta[0], keep, send)
        acc_q[...] = jnp.zeros_like(acc_q)
        acc_k[...] = jnp.zeros_like(acc_k)
        acc_v[...] = jnp.zeros_like(acc_v)

    depth = wq.shape[0]
    xs = x[:, pl.ds(pl.multiple_of(j * depth, depth), depth)]
    acc_q[...] += dot_nn(xs, wq[...])
    acc_k[...] += dot_nn(xs, wk[...])
    acc_v[...] += dot_nn(xs, wv[...])

    @pl.when(j == last)
    def _():
        def turn(raw, gain):
            inverse = lax.rsqrt(jnp.mean(raw * raw, axis=-1, keepdims=True) + EPS)
            normed = raw * inverse * gain
            return (normed * cos[...] + pltpu.roll(normed, HEAD // 2, 1) * sin[...]).astype(BF)

        q_raw[...] = acc_q[...]
        k_raw[...] = acc_k[...]
        for h in range(acc_q.shape[1] // HEAD):
            at = slice(h * HEAD, (h + 1) * HEAD)
            q_out[:, at] = turn(acc_q[:, at], gq[...])
        span = kv_out.shape[2]
        for h in range(acc_k.shape[1] // HEAD):
            at = slice(h * HEAD, (h + 1) * HEAD)
            turned = turn(acc_k[:, at], gk[...])
            for r in range(row_count):
                kv_out[r, 0, :, at] = turned[r * span : (r + 1) * span]
        for r in range(row_count):
            kv_out[r, 1] = acc_v[r * span : (r + 1) * span, :].astype(BF)


def qkv_call(meta, row_count, x, weights, gains, tables):
    tokens, width = x.shape
    nq, nk = weights[0].shape[1], weights[1].shape[1]
    depth = width // 4
    row = lambda n: pl.BlockSpec((depth, n), lambda j, *_: (j, 0))
    kv = (row_count, 2, tokens // row_count, nk)
    return call(
        functools.partial(qkv_kernel, row_count),
        (4,),
        [whole((tokens, width)), row(nq), row(nk), row(nk)]
        + [whole((1, HEAD))] * 2
        + [whole((tokens, HEAD))] * 2,
        [whole((tokens, nq)), whole(kv), whole((tokens, nq)), whole((tokens, nk))]
        + [whole((tokens, width // 2))] * 2,
        [hbm((tokens, nq), BF), hbm(kv, BF), hbm((tokens, nq), F32), hbm((tokens, nk), F32)]
        + [hbm((tokens, width // 2), BF)] * 2,
        [pltpu.VMEM((tokens, nq), F32), pltpu.VMEM((tokens, nk), F32), pltpu.VMEM((tokens, nk), F32)],
        (meta, x, *weights, *gains, *tables),
        40,
    )


def stack_heads(ref, group):
    return jnp.concatenate([ref[:, h * HEAD : (h + 1) * HEAD] for h in range(group)], axis=0)


def bounds(meta, at, row, docs, span, group):
    place = meta[at] + lax.broadcasted_iota(I32, (span, 1), 0)
    begin = jnp.zeros_like(place)
    for d in range(docs):
        start = meta[at + 1 + row * docs + d]
        begin = jnp.where(place >= start, start, begin)
    return jnp.concatenate([place] * group, axis=0), jnp.concatenate([begin] * group, axis=0)


def attend_kernel(slot_count, docs, group, scale, meta, *refs):
    q_ref, refs = refs[0], refs[1:]
    keys, refs = refs[:slot_count], refs[slot_count:]
    wo = refs[0]
    o_out, lse_out, part_out = refs[1:4]
    scores, acc = refs[4:]
    r, g, last = pl.program_id(0), pl.program_id(1), pl.num_programs(1) - 1
    first = r * slot_count
    bases = pl.num_programs(0) * slot_count
    span = q_ref.shape[0]
    queries = stack_heads(q_ref, group)
    high, low = bounds(meta, bases + slot_count + 1, r, docs, span, group)
    k_place = lax.broadcasted_iota(I32, (1, span), 1)
    top = jnp.full((group * span, HEAD), MASKED, F32)

    for s in range(slot_count):

        def some(top, s=s):
            raw = dot_nt(queries, keys[s][0, 0]) * scale
            place = k_place + meta[bases + s]
            kept = jnp.where((place >= low) & (place <= high), raw, MASKED)
            scores[s] = kept
            for c in range(span // HEAD):
                top = jnp.maximum(top, kept[:, c * HEAD : (c + 1) * HEAD])
            return top

        top = lax.cond(meta[first + s] > 0, some, lambda t: t, top)

    peak = jnp.max(top, axis=-1, keepdims=True)
    total = jnp.zeros((group * span, HEAD), F32)
    out = jnp.zeros((group * span, HEAD), F32)
    for s in range(slot_count):

        def more(carry, s=s):
            total, out = carry
            power = jnp.exp2(scores[s] - peak)
            for c in range(span // HEAD):
                total = total + power[:, c * HEAD : (c + 1) * HEAD]
            return total, out + dot_nn(power.astype(BF), keys[s][0, 1])

        total, out = lax.cond(meta[first + s] > 0, more, lambda t: t, (total, out))

    total = jnp.sum(total, axis=-1, keepdims=True)
    lse_out[0, 0] = peak + jnp.log2(total)
    out = (out / total).astype(BF)
    out = jnp.concatenate([out[h * span : (h + 1) * span] for h in range(group)], axis=1)
    o_out[...] = out
    part = dot_nn(out, wo[...])

    @pl.when(g == 0)
    def _():
        acc[...] = part

    @pl.when(g > 0)
    def _():
        acc[...] += part

    @pl.when(g == last)
    def _():
        part_out[...] = acc[...].astype(BF)


def attend_call(meta, docs, queries, kv_slots, wo):
    slot_count = len(kv_slots)
    tokens, nq = queries.shape
    row_count, _, span, nk = kv_slots[0].shape
    heads, group = nk // HEAD, nq // nk
    width = wo.shape[1]
    wide = group * HEAD
    rows = pl.BlockSpec((span, wide), lambda r, g, *_: (r, g))
    return call(
        functools.partial(attend_kernel, slot_count, docs, group, HEAD**-0.5 * LOG2E),
        (row_count, heads),
        [rows]
        + [pl.BlockSpec((1, 2, span, HEAD), lambda r, g, *_: (r, 0, 0, g))] * slot_count
        + [pl.BlockSpec((wide, width), lambda r, g, *_: (g, 0))],
        [
            rows,
            pl.BlockSpec((1, 1, group * span, 1), lambda r, g, *_: (r, g, 0, 0)),
            pl.BlockSpec((span, width), lambda r, g, *_: (r, 0)),
        ],
        [hbm((tokens, nq), BF), hbm((row_count, heads, group * span, 1), F32), hbm((tokens, width), BF)],
        [pltpu.VMEM((slot_count, group * span, span), F32), pltpu.VMEM((span, width), F32)],
        (meta, queries, *kv_slots, wo),
        40,
    )


def ff_kernel(meta, x, og, wg, wu, wd, out, keep, send):
    @pl.when(pl.program_id(0) == 0)
    def _():
        half_out(x, meta[0], keep, send)

    gate = dot_nn(x[...], wg[...])
    up = dot_nn(x[...], wu[...])
    upstream = dot_nt(og[...], wd[...])
    sigmoid = 1.0 / (1.0 + jnp.exp(-gate))
    silu = gate * sigmoid
    out[0] = (silu * up).astype(BF)
    out[1] = (upstream * up * sigmoid * (1.0 + gate * (1.0 - sigmoid))).astype(BF)
    out[2] = (upstream * silu).astype(BF)


def ff_call(meta, x, og, wg, wu, wd, after):
    tokens, width = x.shape
    hidden = wg.shape[1]
    block = 256
    column = pl.BlockSpec((width, block), lambda j, *_: (0, j))
    return call(
        ff_kernel,
        (hidden // block,),
        [whole((tokens, width))] * 2 + [column, column, pl.BlockSpec((block, width), lambda j, *_: (j, 0))],
        [pl.BlockSpec((3, tokens, block), lambda j, *_: (0, 0, j))] + [whole((tokens, width // 2))] * 2,
        [hbm((3, tokens, hidden), BF)] + [hbm((tokens, width // 2), BF)] * 2,
        [],
        (meta, x, og, wg, wu, wd),
        48,
        after=after,
    )


def ff_back_kernel(gate, up, wg, wu, out):
    out[...] = (dot_nt(gate[0], wg[...]) + dot_nt(up[0], wu[...])).astype(BF)


def ff_back_call(planes, wg, wu):
    _, tokens, hidden = planes.shape
    width = wg.shape[0]
    block = 512
    row = pl.BlockSpec((block, hidden), lambda j: (j, 0))
    plane = lambda n: pl.BlockSpec((1, tokens, hidden), lambda j: (n, 0, 0))
    return call(
        ff_back_kernel,
        (width // block,),
        [plane(1), plane(2), row, row],
        [pl.BlockSpec((tokens, block), lambda j: (0, j))],
        [hbm((tokens, width), BF)],
        [],
        (planes, planes, wg, wu),
        40,
        prefetch=0,
    )[0]


def ff_out_kernel(hm, wd, out):
    out[...] = dot_nn(hm[0], wd[...]).astype(BF)


def ff_out_call(planes, wd):
    _, tokens, hidden = planes.shape
    width = wd.shape[1]
    block = 512
    return call(
        ff_out_kernel,
        (width // block,),
        [pl.BlockSpec((1, tokens, hidden), lambda j: (0, 0, 0)), pl.BlockSpec((hidden, block), lambda j: (0, j))],
        [pl.BlockSpec((tokens, block), lambda j: (0, j))],
        [hbm((tokens, width), BF)],
        [],
        (planes, wd),
        32,
        prefetch=0,
    )[0]


def norm_back(turned, raw, gain, cos, sin):
    upstream = turned * cos - pltpu.roll(turned, HEAD // 2, 1) * sin
    inverse = lax.rsqrt(jnp.mean(raw * raw, axis=-1, keepdims=True) + EPS)
    scaled = upstream * gain
    through = inverse * scaled - raw * (inverse * inverse * inverse) * jnp.mean(
        raw * scaled, axis=-1, keepdims=True
    )
    return through.astype(BF), jnp.sum(upstream * raw * inverse, axis=0, keepdims=True)


def attend_back_kernel(slot_count, docs, group, scale, meta, *refs):
    bg, wo, q_ref, refs = refs[0], refs[1], refs[2], refs[3:]
    keys, refs = refs[:slot_count], refs[slot_count:]
    o_ref, lse_ref, q_raw, gq, cos, sin = refs[:6]
    dq_out, even_out, odd_low, odd_high, gain_out, keep, send = refs[6:]
    r, g = pl.program_id(0), pl.program_id(1)
    first = r * slot_count
    bases = pl.num_programs(0) * slot_count

    @pl.when(g == 0)
    def _():
        half_out(bg, meta[bases + slot_count], keep, send)

    @pl.when((r == 0) & (g == 0))
    def _():
        gain_out[...] = jnp.zeros_like(gain_out)

    span = q_ref.shape[0]
    d_out = dot_nt(bg[...], wo[...]).astype(BF)
    d_out = jnp.concatenate([d_out[:, h * HEAD : (h + 1) * HEAD] for h in range(group)], axis=0)
    o_rows = stack_heads(o_ref, group)
    queries = stack_heads(q_ref, group)
    centre = jnp.sum(d_out.astype(F32) * o_rows.astype(F32), axis=-1, keepdims=True)
    lse = lse_ref[0, 0]
    high, low = bounds(meta, bases + slot_count + 1, r, docs, span, group)
    k_place = lax.broadcasted_iota(I32, (1, span), 1)
    dq = jnp.zeros((group * span, HEAD), F32)
    for s in range(slot_count):
        half = slot_count // 4
        if s % 2 == 0:
            out = even_out.at[s // 2, 0]
        else:
            out = (odd_low if s // 2 < half else odd_high).at[s // 2 % half, 0]

        def some(dq, s=s, out=out):
            raw = dot_nt(queries, keys[s][0, 0]) * (scale * LOG2E)
            place = k_place + meta[bases + s]
            probs = jnp.where((place >= low) & (place <= high), jnp.exp2(raw - lse), 0.0)
            d_probs = dot_nt(d_out, keys[s][0, 1])
            d_score = (probs * (d_probs - centre)).astype(BF)
            out[0] = (dot_tn(d_score, queries) * scale).astype(BF)
            out[1] = dot_tn(probs.astype(BF), d_out).astype(BF)
            return dq + dot_nn(d_score, keys[s][0, 0])

        def none(dq, out=out):
            out[...] = jnp.zeros(out.shape, BF)
            return dq

        dq = lax.cond(meta[first + s] > 0, some, none, dq)

    gain = gq[...]
    gain_total = jnp.zeros((1, HEAD), F32)
    for h in range(group):
        rows = dq[h * span : (h + 1) * span] * scale
        d_raw, part = norm_back(rows, q_raw[:, h * HEAD : (h + 1) * HEAD], gain, cos[...], sin[...])
        dq_out[:, h * HEAD : (h + 1) * HEAD] = d_raw
        gain_total = gain_total + part
    gain_out[...] += gain_total


def attend_back_call(meta, docs, bg, wo, queries, kv_slots, attended, lse, q_raw, gq, tables, after):
    slot_count = len(kv_slots)
    tokens, width = bg.shape
    nq = queries.shape[1]
    row_count, _, span, nk = kv_slots[0].shape
    heads, group = nk // HEAD, nq // nk
    wide = group * HEAD
    rows = pl.BlockSpec((span, wide), lambda r, g, *_: (r, g))
    by_row = lambda n: pl.BlockSpec((span, n), lambda r, g, *_: (r, 0))
    kv_out = lambda n: pl.BlockSpec((n, 1, 2, span, HEAD), lambda r, g, *_: (0, r, 0, 0, g))
    kv_shape = lambda n: hbm((n, row_count, 2, span, nk), BF)
    half, quarter = slot_count // 2, slot_count // 4
    return call(
        functools.partial(attend_back_kernel, slot_count, docs, group, HEAD**-0.5),
        (row_count, heads),
        [by_row(width), pl.BlockSpec((wide, width), lambda r, g, *_: (g, 0)), rows]
        + [pl.BlockSpec((1, 2, span, HEAD), lambda r, g, *_: (r, 0, 0, g))] * slot_count
        + [rows, pl.BlockSpec((1, 1, group * span, 1), lambda r, g, *_: (r, g, 0, 0))]
        + [rows, whole((1, HEAD)), by_row(HEAD), by_row(HEAD)],
        [rows, kv_out(half), kv_out(quarter), kv_out(quarter), whole((1, HEAD)), by_row(width // 2), by_row(width // 2)],
        [
            hbm((tokens, nq), BF),
            kv_shape(half),
            kv_shape(quarter),
            kv_shape(quarter),
            sds((1, HEAD), F32),
            hbm((tokens, width // 2), BF),
            hbm((tokens, width // 2), BF),
        ],
        [],
        (meta, bg, wo, queries, *kv_slots, attended, lse, q_raw, gq, *tables),
        40,
        after=after,
    )


def key_back_kernel(count, row_count, *refs):
    pieces, refs = refs[:count], refs[count:]
    dq_ref, k_raw, gk, cos, sin, all_out, gain_out = refs
    span, nk = pieces[0].shape[2:]
    nq = dq_ref.shape[1]
    all_out[:, :nq] = dq_ref[...]
    gain_total = jnp.zeros((1, HEAD), F32)
    for r in range(row_count):
        rows = slice(r * span, (r + 1) * span)
        for h in range(nk // HEAD):
            at = slice(h * HEAD, (h + 1) * HEAD)
            turned = sum(p[r, 0, :, at].astype(F32) for p in pieces)
            d_raw, part = norm_back(turned, k_raw[rows, at], gk[...], cos[rows], sin[rows])
            all_out[rows, nq + h * HEAD : nq + (h + 1) * HEAD] = d_raw
            gain_total = gain_total + part
        all_out[rows, nq + nk :] = sum(p[r, 1].astype(F32) for p in pieces).astype(BF)
    gain_out[...] = gain_total


def key_back_call(pieces, dq, k_raw, gk, tables, after):
    tokens, nq = dq.shape
    nk = k_raw.shape[1]
    return call(
        functools.partial(key_back_kernel, len(pieces), pieces[0].shape[0]),
        (1,),
        [whole(pieces[0].shape)] * len(pieces)
        + [whole((tokens, nq)), whole((tokens, nk)), whole((1, HEAD)), whole((tokens, HEAD)), whole((tokens, HEAD))],
        [whole((tokens, nq + 2 * nk)), whole((1, HEAD))],
        [hbm((tokens, nq + 2 * nk), BF), hbm((1, HEAD), F32)],
        [],
        (*pieces, dq, k_raw, gk, *tables),
        40,
        prefetch=0,
        after=after,
    )


def back_kernel(grads, wq, wk, wv, out):
    nq, nk = wq.shape[1], wk.shape[1]
    part = (
        dot_nt(grads[:, :nq], wq[...])
        + dot_nt(grads[:, nq : nq + nk], wk[...])
        + dot_nt(grads[:, nq + nk :], wv[...])
    )
    out[...] = part.astype(BF)


def back_call(grads, weights):
    tokens, cols = grads.shape
    width = weights[0].shape[0]
    block = width // 4
    return call(
        back_kernel,
        (4,),
        [whole((tokens, cols))] + [pl.BlockSpec((block, w.shape[1]), lambda j: (j, 0)) for w in weights],
        [pl.BlockSpec((tokens, block), lambda j: (0, j))],
        [hbm((tokens, width), BF)],
        [],
        (grads, *weights),
        40,
        prefetch=0,
    )[0]


def turn_rows(ids, parts, left_refs, turned):
    tokens, rows = left_refs[0].shape
    part = turned.shape[0] // parts
    for k, ref in enumerate(left_refs):
        for n in range(parts):
            block = ref[:, pl.ds(pl.multiple_of(ids[n] * part, HEAD), part)]
            turned[n * part : (n + 1) * part, k * tokens : (k + 1) * tokens] = block.T


def put_rows(total, outs, at):
    part = total.shape[0] // len(outs)
    for n, out in enumerate(outs):
        out[at] = total[n * part : (n + 1) * part].astype(BF)


def ff_grad_kernel(ids, og0, og1, x0, x1, p0, p1, *refs):
    outs, turned = refs[:-1], refs[-1]

    @pl.when(pl.program_id(0) == 0)
    def _():
        turn_rows(ids, len(outs), (og0, og1), turned.at[0])
        turn_rows(ids, len(outs), (x0, x1), turned.at[1])

    for n in range(3):
        right = jnp.concatenate([p0[n], p1[n]], axis=0)
        put_rows(dot_nn(turned[min(n, 1)], right), outs, n)


def ff_grad_call(ids, ogs, xs, planes):
    tokens, rows = xs[0].shape
    hidden = planes[0].shape[2]
    wide = next(w for w in (512, 384, 256, 128) if hidden % w == 0)
    part = rows // 4
    count = ids.shape[0]
    return call(
        ff_grad_kernel,
        (hidden // wide,),
        [whole((tokens, rows))] * 4 + [pl.BlockSpec((3, tokens, wide), lambda c, ids: (0, 0, c))] * 2,
        [pl.BlockSpec((3, part, wide), lambda c, ids: (0, 0, c))] * count,
        [hbm((3, part, hidden), BF)] * count,
        [pltpu.VMEM((2, count * part, 2 * tokens), BF)],
        (ids, *ogs, *xs, *planes),
        48,
    )


def attn_grad_kernel(steps, ids, x0, x1, b0, b1, g0, g1, o0, o1, *refs):
    outs, turned = refs[:-1], refs[-1]
    c = pl.program_id(0)

    @pl.when(c == 0)
    def _():
        turn_rows(ids, len(outs), (x0, x1), turned)

    @pl.when(c == steps)
    def _():
        turn_rows(ids, len(outs), (b0, b1), turned)

    @pl.when(c < steps)
    def _():
        put_rows(dot_nn(turned[...], jnp.concatenate([g0[...], g1[...]], axis=0)), outs, 0)

    @pl.when(c >= steps)
    def _():
        put_rows(dot_nn(turned[...], jnp.concatenate([o0[...], o1[...]], axis=0)), outs, 0)


def attn_grad_call(ids, xs, bs, grads, outs):
    tokens, rows = xs[0].shape
    wide = outs[0].shape[1] if grads[0].shape[1] % outs[0].shape[1] == 0 else HEAD
    steps = grads[0].shape[1] // wide
    more = outs[0].shape[1] // wide
    part = rows // 4
    count = ids.shape[0]
    cols = (steps + more) * wide
    return call(
        functools.partial(attn_grad_kernel, steps),
        (steps + more,),
        [whole((tokens, rows))] * 4
        + [pl.BlockSpec((tokens, wide), lambda c, ids: (0, jnp.minimum(c, steps - 1)))] * 2
        + [pl.BlockSpec((tokens, wide), lambda c, ids: (0, jnp.maximum(c - steps, 0)))] * 2,
        [pl.BlockSpec((1, part, wide), lambda c, ids: (0, 0, c))] * count,
        [hbm((1, part, cols), BF)] * count,
        [pltpu.VMEM((count * part, 2 * tokens), BF)],
        (ids, *xs, *bs, *grads, *outs),
        48,
    )


def split_kernel(bits, keep_a, got_a, keep_b, got_b, send_a, next_a, send_b, next_b):
    j = pl.program_id(0)

    def put(out, keep, got):
        out[...] = (keep[...].astype(F32) + got[...].astype(F32)).astype(BF)

    @pl.when(j == 0)
    def _():
        put(send_a, keep_a, got_a)
        put(send_b, keep_b, got_b)

    @pl.when(j == 1)
    def _():
        put(next_a, keep_a, got_a)
        put(next_b, keep_b, got_b)


def split_call(bits, keeps, gots, after):
    *lead, rows, cols = keeps[0].shape
    zeros = (0,) * len(lead)
    half = (*lead, rows // 2, cols)
    part = lambda f: pl.BlockSpec(half, lambda j, bits: (*zeros, jnp.where(j == 0, 1 - bits[f], bits[f]), 0))
    send_a, next_a, send_b, next_b = call(
        split_kernel,
        (2,),
        [part(0), part(0), part(1), part(1)],
        [whole(half)] * 4,
        [hbm(half, BF)] * 4,
        [],
        (bits, keeps[0], gots[0], keeps[1], gots[1]),
        40,
        after=after,
    )
    return (send_a, send_b), (next_a, next_b)


def sum_kernel(bits, *refs):
    count = (len(refs) - 2) // 2
    for f, out in enumerate(refs[2 * count :]):
        total = refs[f * count][...].astype(F32)
        for ref in refs[f * count + 1 : (f + 1) * count]:
            total = total + ref[...].astype(F32)
        out[...] = total.astype(BF)


def sum_call(bits, flows, after=()):
    rows = min(v.shape[1] for v in flows[0])
    planes, _, cols = flows[0][0].shape
    block = (planes, rows // 2, cols)

    def part(v, f):
        long = v.shape[1] > rows
        return pl.BlockSpec(block, lambda j, bits: (0, j + (2 * bits[f] if long else 0), 0))

    return call(
        sum_kernel,
        (2,),
        [part(v, f) for f, vs in enumerate(flows) for v in vs],
        [pl.BlockSpec(block, lambda j, bits: (0, j, 0))] * 2,
        [hbm((planes, rows, cols), BF)] * 2,
        [],
        (bits, *flows[0], *flows[1]),
        40,
        after=after,
    )


def half_sum_call(bits, keeps, gots):
    planes, rows, cols = keeps[0].shape
    block = (planes, rows // 4, cols)
    part = lambda f: pl.BlockSpec(block, lambda j, bits: (0, j + 2 * bits[f], 0))
    return call(
        sum_kernel,
        (2,),
        [part(0), part(0), part(1), part(1)],
        [pl.BlockSpec(block, lambda j, bits: (0, j, 0))] * 2,
        [hbm((planes, rows // 2, cols), BF)] * 2,
        [],
        (bits, keeps[0], gots[0], keeps[1], gots[1]),
        40,
    )


def widen_kernel(count, planes, turned, table, *refs):
    pieces, outs = refs[: count * planes], refs[count * planes :]

    def put(refs):
        at, plane = 0, 0
        for k, out in enumerate(outs):
            if k in turned:
                wide = out.shape[0]
                out[...] = refs[plane][0, :, at : at + wide].T.astype(F32)
            else:
                wide = out.shape[1]
                out[...] = refs[plane][0, :, at : at + wide].astype(F32)
            at += wide
            if at == refs[plane].shape[2]:
                at, plane = 0, plane + 1

    for k in range(count):

        @pl.when(pl.program_id(0) == k)
        def _(k=k):
            put(pieces[k * planes : (k + 1) * planes])


def widen_call(table, pieces, planes, shapes, turned, after):
    _, rows, cols = pieces[0].shape
    count = len(pieces)
    place = lambda n: pl.BlockSpec((1, rows, cols), lambda j, t: (n, 0, 0), pipeline_mode=pl.Buffered(1))
    by_row = lambda s: pl.BlockSpec((rows, s[1]), lambda j, t: (t[j], 0))
    by_col = lambda s: pl.BlockSpec((s[0], rows), lambda j, t: (0, t[j]))
    return call(
        functools.partial(widen_kernel, count, len(planes), turned),
        (count,),
        [place(n) for _ in range(count) for n in planes],
        [by_col(s) if k in turned else by_row(s) for k, s in enumerate(shapes)],
        [hbm(s, F32) for s in shapes],
        [],
        (table, *(p for p in pieces for _ in planes)),
        56,
        after=after,
    )


def norm_kernel(x, gain, out):
    value = x[...].astype(F32)
    inverse = lax.rsqrt(jnp.mean(value * value, axis=-1, keepdims=True) + EPS)
    out[...] = (value * inverse * gain[...]).astype(BF)


def norm_call(x, gain):
    return call(
        norm_kernel,
        (1,),
        [whole(x.shape), whole(gain.shape)],
        [whole(x.shape)],
        [hbm(x.shape, BF)],
        [],
        (x, gain),
        24,
        prefetch=0,
    )[0]


def middle_kernel(x, got, gain, middle, out):
    value = x[...].astype(F32) + got[...].astype(F32)
    inverse = lax.rsqrt(jnp.mean(value * value, axis=-1, keepdims=True) + EPS)
    middle[...] = value
    out[...] = (value * inverse * gain[...]).astype(BF)


def middle_call(x, got, gain, after):
    return call(
        middle_kernel,
        (1,),
        [whole(x.shape), whole(x.shape), whole(gain.shape)],
        [whole(x.shape)] * 2,
        [hbm(x.shape, F32), hbm(x.shape, BF)],
        [],
        (x, got, gain),
        24,
        prefetch=0,
        after=after,
    )


def norm_grad_kernel(x, got, base, gain, *outs):
    value, upstream = x[...].astype(F32), got[...].astype(F32)
    inverse = lax.rsqrt(jnp.mean(value * value, axis=-1, keepdims=True) + EPS)
    scaled = upstream * gain[...]
    through = inverse * scaled - value * (inverse * inverse * inverse) * jnp.mean(
        value * scaled, axis=-1, keepdims=True
    )
    total = base[...].astype(F32) + through
    outs[0][...] = total
    outs[1][...] = jnp.sum(upstream * value * inverse, axis=0, keepdims=True)
    if len(outs) > 2:
        outs[2][...] = total.astype(BF)


def norm_grad_call(x, got, base, gain, low, after=()):
    return call(
        norm_grad_kernel,
        (1,),
        [whole(x.shape)] * 3 + [whole(gain.shape)],
        [whole(x.shape), whole(gain.shape)] + [whole(x.shape)] * low,
        [hbm(x.shape, F32), hbm(gain.shape, F32)] + [hbm(x.shape, BF)] * low,
        [],
        (x, got, base, gain),
        24,
        prefetch=0,
        after=after,
    )


class WeightSum:
    def __init__(self, masks):
        self.flows = (masks, masks[::-1])
        seq = lax.axis_index("seq")
        self.core = seq & 1
        self.bits = [jnp.stack([(seq & m[k]) // m[k] for m in self.flows]) for k in range(len(masks))]
        base = jnp.array([0, 2], I32)
        self.send_ids, self.keep_ids = base + 1 - self.bits[0], base + self.bits[0]
        self.level = 0

    def swap_level(self, sends):
        self.gots = [swap(s, "seq", m[self.level]) for s, m in zip(sends, self.flows)]
        self.level += 1

    def begin(self, sends):
        self.swap_level(sends)

    def middle(self):
        count = len(self.flows[0])
        self.terms = [[k] for k in self.kept]
        while self.level < count:
            bits = self.bits[self.level]
            if self.level < count - 1:
                sends, kept = split_call(bits, self.kept, self.gots, ())
                self.kept = kept
            else:
                sends = half_sum_call(1 - bits, self.kept, self.gots)
                self.terms = [[k, g] for k, g in zip(self.kept, self.gots)]
            self.swap_level(sends)
        self.terms = [t + [g] for t, g in zip(self.terms, self.gots)]

    def last(self, after=()):
        parts = sum_call(self.bits[-1], self.terms, after)
        for level in range(len(self.flows[0]) - 1, 0, -1):
            gots = [swap(p, "seq", m[level]) for p, m in zip(parts, self.flows)]
            parts = [
                jnp.where(self.bits[level][f] == 0, *(jnp.concatenate(v, axis=1) for v in ((p, g), (g, p))))
                for f, (p, g) in enumerate(zip(parts, gots))
            ]
        self.parts = parts
        self.ends = [v for p, m in zip(parts, self.flows) for v in (p, swap(p, "seq", m[0]))]
        self.others = [swap(v, "seq", 1) for v in self.ends]

    def widen(self, planes, shapes, turned, after=()):
        blocks = jnp.stack([h for f in range(2) for h in (2 * f + self.bits[0][f], 2 * f + 1 - self.bits[0][f])])
        table = jnp.concatenate([self.core * 4 + blocks, (1 - self.core) * 4 + blocks])
        return widen_call(table, (*self.ends, *self.others), planes, shapes, turned, after)


def halves(value, core):
    half = value.shape[1] // 2
    return (
        lax.dynamic_slice_in_dim(value, core * half, half, 1),
        lax.dynamic_slice_in_dim(value, (1 - core) * half, half, 1),
    )


def body(
    hidden_in,
    output_grad,
    document_lengths,
    attention_gain,
    query_weight,
    key_weight,
    value_weight,
    query_gain,
    key_gain,
    output_weight,
    feedforward_gain,
    gate_weight,
    up_weight,
    down_weight,
):
    ORDER.clear()
    tp, seqs = lax.axis_size("tp"), lax.axis_size("seq")
    seq_at = lax.axis_index("seq")
    core = seq_at & 1
    row_count, share, width = hidden_in.shape
    span = share * tp
    masks = tuple(1 << b for b in range(1, seqs.bit_length() - 1))

    ends = jnp.stack(
        [jnp.sum(document_lengths[:, : n + 1], axis=1) for n in range(document_lengths.shape[1])], axis=1
    )
    starts = ends - document_lengths
    docs = document_lengths.shape[1]
    places = seq_at * span + jnp.arange(span, dtype=I32)
    inside = (places[None, :, None] >= starts[:, None]) & (places[None, :, None] < ends[:, None])
    begun = jnp.sum(jnp.where(inside, starts[:, None], 0), axis=2)
    slot_seq = jnp.arange(seqs, dtype=I32) ^ seq_at
    needed = (slot_seq <= seq_at)[None] & ((slot_seq + 1)[None] * span > begun[:, :1])
    meta = jnp.concatenate(
        [needed.astype(I32).reshape(-1), slot_seq * span, core[None], places[:1], starts.reshape(-1)]
    )
    frequency = ROPE_BASE ** (-2.0 * jnp.arange(HEAD // 2, dtype=F32) / HEAD)
    angles = (places[None] - begun).reshape(-1, 1).astype(F32) * frequency
    cos, sin = jnp.cos(angles), jnp.sin(angles)
    tables = (jnp.concatenate([cos, cos], 1), jnp.concatenate([-sin, sin], 1))
    core_meta = core[None]
    q_gain, k_gain = query_gain[None], key_gain[None]
    qkv_weights = (query_weight, key_weight, value_weight)

    flat = lambda v: v.reshape(-1, width)
    hidden, upward = flat(hidden_in), flat(output_grad)
    attn_gain, ff_gain = attention_gain[None], feedforward_gain[None]
    shares = lambda v: v.reshape(row_count, share, width)
    normed1 = gather_tp(shares(norm_call(hidden, attn_gain)))
    queries, kv, q_raw, k_raw, n1_keep, n1_send = qkv_call(
        core_meta, row_count, normed1, qkv_weights, (q_gain, k_gain), tables
    )
    grads = gather_tp(output_grad)
    kv_slots = []
    for value in [kv] + [swap(kv, "seq", m) for m in range(2, seqs, 2)]:
        kv_slots += [value, swap(value, "seq", 1)]
    attended, lse, o_part = attend_call(meta, docs, queries, kv_slots, output_weight)

    def both(own, sent=None):
        return [own, swap(own if sent is None else sent, "seq", 1)]

    o_both = both(attended)
    n1_both = both(n1_keep, n1_send)
    middle, normed2 = middle_call(hidden, flat(scatter_tp(o_part, row_count)), ff_gain, (grads,))
    grads_both = both(*halves(grads, core))
    normed2 = gather_tp(shares(normed2))
    planes, n2_keep, n2_send = ff_call(
        core_meta, normed2, grads, gate_weight, up_weight, down_weight, (grads_both[1], o_both[1], n1_both[1])
    )
    planes_both, n2_both = both(planes), both(n2_keep, n2_send)
    n2_got = scatter_tp(ff_back_call(planes, gate_weight, up_weight), row_count)

    ff = WeightSum(masks)
    ff.begin(ff_grad_call(ff.send_ids, grads_both, n2_both, planes_both))
    ff.kept = ff_grad_call(ff.keep_ids, grads_both, n2_both, planes_both)
    middle_grad, ff_gain_grad, branch = norm_grad_call(middle, flat(n2_got), upward, ff_gain, True, ff.gots)
    branch = gather_tp(shares(branch))
    ff.middle()
    ff_got = scatter_tp(ff_out_call(planes, down_weight), row_count)
    ff.last()
    dq, even, odd_low, odd_high, q_gain_grad, b_keep, b_send = attend_back_call(
        meta,
        docs,
        branch,
        output_weight,
        queries,
        kv_slots,
        attended,
        lse,
        q_raw,
        q_gain,
        tables,
        ff.parts,
    )
    odd = [v[k] for v in (swap(odd_low, "seq", 1), swap(odd_high, "seq", 1)) for k in range(seqs // 4)]
    chip = [(even[k].astype(F32) + odd[k].astype(F32)).astype(BF) for k in range(seqs // 2)]
    pieces = [chip[0]] + [swap(chip[m // 2], "seq", m) for m in range(2, seqs, 2)]
    bg_both = both(b_keep, b_send)
    all_grad, k_gain_grad = key_back_call(pieces, dq, k_raw, k_gain, tables, (*ff.ends, ff_got, bg_both[1]))
    all_both = both(all_grad)
    n1_part = back_call(all_grad, qkv_weights)
    n1_got = scatter_tp(n1_part, row_count)
    attn = WeightSum(masks)
    ids = jnp.concatenate([attn.send_ids, attn.keep_ids])
    parts = attn_grad_call(ids, n1_both, bg_both, all_both, o_both)
    attn.kept = parts[2:]
    attn.begin(parts[:2])
    gate_out, up_out = ff.widen((1, 2), [gate_weight.shape, up_weight.shape], ())
    attn.middle()
    input_grad, attn_gain_grad = norm_grad_call(hidden, flat(n1_got), middle_grad, attn_gain, False)
    gains = jnp.concatenate(
        [v.reshape(-1) for v in (attn_gain_grad, ff_gain_grad, q_gain_grad, k_gain_grad)]
    ).reshape(-1, HEAD)
    sums = [gains]
    for axis, size in (("tp", tp), ("seq", seqs)):
        for level in range(size.bit_length() - 1):
            sums.append(sums[-1] + swap(sums[-1], axis, 1 << level))
    gains = sums[-1]
    input_grad = shares(input_grad)
    block_out = shares((middle + flat(ff_got).astype(F32)).astype(BF))
    attn.last()
    (down_out,) = ff.widen((0,), [down_weight.shape], (0,))
    query_out, key_out, value_out, output_out = attn.widen(
        (0,), [w.shape for w in (*qkv_weights, output_weight)], (3,), sums[-1:]
    )
    gains = gains.reshape(-1)
    return (
        block_out,
        input_grad,
        gains[:width],
        query_out,
        key_out,
        value_out,
        gains[2 * width : 2 * width + HEAD],
        gains[2 * width + HEAD :],
        output_out,
        gains[width : 2 * width],
        gate_out,
        up_out,
        down_out,
    )


def solution(mesh):
    tokens, columns, rows = P(None, ("seq", "tp"), None), P(None, "tp"), P("tp", None)
    in_specs = (
        tokens,
        tokens,
        P(),
        P(),
        columns,
        columns,
        columns,
        P(),
        P(),
        rows,
        P(),
        columns,
        columns,
        rows,
    )
    out_specs = (
        tokens,
        tokens,
        P(),
        columns,
        columns,
        columns,
        P(),
        P(),
        rows,
        P(),
        columns,
        columns,
        rows,
    )
    return jax.shard_map(body, mesh=mesh, in_specs=in_specs, out_specs=out_specs, check_vma=False)
```

```python
import functools
import math

import jax
import jax.numpy as jnp
from jax import lax
from jax.experimental import pallas as pl
from jax.experimental.pallas import tpu as pltpu
from jax.sharding import PartitionSpec as P

HEAD = 128
EPS = 1e-06
ROPE_BASE = 1000000.0
MASKED = -1e30
LOG2E = math.log2(math.e)
BF = jnp.bfloat16
F32 = jnp.float32
I32 = jnp.int32


def sds(shape, dtype):
    return jax.ShapeDtypeStruct(shape, dtype)


def hbm(shape, dtype):
    return pltpu.HBM(shape, dtype)


def whole(shape):
    return pl.BlockSpec(shape, lambda *_: (0,) * len(shape))


def dot_nn(a, b):
    return lax.dot_general(a, b, (((1,), (0,)), ((), ())), preferred_element_type=F32)


def dot_nt(a, b):
    return lax.dot_general(a, b, (((1,), (1,)), ((), ())), preferred_element_type=F32)


def dot_tn(a, b):
    return lax.dot_general(a, b, (((0,), (0,)), ((), ())), preferred_element_type=F32)


def in_hbm(value):
    return pltpu.with_memory_space_constraint(value, pltpu.HBM)


def call(body, grid, in_specs, out_specs, out_shape, scratch, operands, mib, prefetch=1, after=(), free=False, aliases={}):
    after = (*ORDER, *after)
    at, extra = prefetch + len(in_specs), len(after)

    def run(*refs):
        return body(*refs[:at], *refs[at + extra :])

    if not free:
        operands = operands[:prefetch] + tuple(in_hbm(v) for v in operands[prefetch:])
    outs = pl.pallas_call(
        run,
        grid_spec=pltpu.PrefetchScalarGridSpec(
            num_scalar_prefetch=prefetch,
            grid=grid,
            in_specs=in_specs + [pl.BlockSpec(memory_space=pl.ANY)] * extra,
            out_specs=out_specs,
            scratch_shapes=scratch,
        ),
        out_shape=out_shape,
        input_output_aliases=aliases,
        compiler_params=pltpu.CompilerParams(
            vmem_limit_bytes=mib << 20, dimension_semantics=("arbitrary",) * len(grid)
        ),
        cost_estimate=pl.CostEstimate(flops=1, bytes_accessed=1, transcendentals=0),
    )(*operands, *(in_hbm(v) for v in after))
    ORDER[:] = [outs[0]]
    return outs


ORDER = []


def flip(axis, mask):
    return [(i, i ^ mask) for i in range(lax.axis_size(axis))]


def swap(value, axis, mask):
    return lax.ppermute(value, axis, flip(axis, mask))


def sum_copies(value, axis, masks):
    while masks:
        if len(masks) % 2:
            value = value + swap(value, axis, masks[0])
            masks = masks[1:]
        else:
            a, b = masks[:2]
            value = (value + swap(value, axis, a)) + (swap(value, axis, b) + swap(value, axis, a | b))
            masks = masks[2:]
    return value


def gather_tp(share):
    rows, _, width = share.shape
    return lax.all_gather(share, "tp", axis=1, tiled=True).reshape(-1, width)


def scatter_tp(part, row_count):
    part = part.reshape(row_count, -1, part.shape[1])
    return lax.psum_scatter(part, "tp", scatter_dimension=1, tiled=True)


def half_out(x_ref, core, keep_ref, send_ref):
    half = keep_ref.shape[1]
    keep_ref[...] = x_ref[:, pl.ds(pl.multiple_of(core * half, half), half)]
    send_ref[...] = x_ref[:, pl.ds(pl.multiple_of((1 - core) * half, half), half)]


def qkv_kernel(row_count, meta, x, wq, wk, wv, gq, gk, cos, sin, q_out, kv_out, q_raw, k_raw, keep, send, acc_q, acc_k, acc_v):
    j, last = pl.program_id(0), pl.num_programs(0) - 1

    @pl.when(j == 0)
    def _():
        half_out(x, meta[0], keep, send)
        acc_q[...] = jnp.zeros_like(acc_q)
        acc_k[...] = jnp.zeros_like(acc_k)
        acc_v[...] = jnp.zeros_like(acc_v)

    depth = wq.shape[0]
    xs = x[:, pl.ds(pl.multiple_of(j * depth, depth), depth)]
    acc_q[...] += dot_nn(xs, wq[...])
    acc_k[...] += dot_nn(xs, wk[...])
    acc_v[...] += dot_nn(xs, wv[...])

    @pl.when(j == last)
    def _():
        def turn(raw, gain):
            inverse = lax.rsqrt(jnp.mean(raw * raw, axis=-1, keepdims=True) + EPS)
            normed = raw * inverse * gain
            return (normed * cos[...] + pltpu.roll(normed, HEAD // 2, 1) * sin[...]).astype(BF)

        q_raw[...] = acc_q[...]
        k_raw[...] = acc_k[...]
        for h in range(acc_q.shape[1] // HEAD):
            at = slice(h * HEAD, (h + 1) * HEAD)
            q_out[:, at] = turn(acc_q[:, at], gq[...])
        span = kv_out.shape[2]
        for h in range(acc_k.shape[1] // HEAD):
            at = slice(h * HEAD, (h + 1) * HEAD)
            turned = turn(acc_k[:, at], gk[...])
            for r in range(row_count):
                kv_out[r, 0, :, at] = turned[r * span : (r + 1) * span]
        for r in range(row_count):
            kv_out[r, 1] = acc_v[r * span : (r + 1) * span, :].astype(BF)


def qkv_call(meta, row_count, x, weights, gains, tables):
    tokens, width = x.shape
    nq, nk = weights[0].shape[1], weights[1].shape[1]
    depth = width // 4
    row = lambda n: pl.BlockSpec((depth, n), lambda j, *_: (j, 0))
    kv = (row_count, 2, tokens // row_count, nk)
    return call(
        functools.partial(qkv_kernel, row_count),
        (4,),
        [whole((tokens, width)), row(nq), row(nk), row(nk)]
        + [whole((1, HEAD))] * 2
        + [whole((tokens, HEAD))] * 2,
        [whole((tokens, nq)), whole(kv), whole((tokens, nq)), whole((tokens, nk))]
        + [whole((tokens, width // 2))] * 2,
        [hbm((tokens, nq), BF), hbm(kv, BF), hbm((tokens, nq), F32), hbm((tokens, nk), F32)]
        + [hbm((tokens, width // 2), BF)] * 2,
        [pltpu.VMEM((tokens, nq), F32), pltpu.VMEM((tokens, nk), F32), pltpu.VMEM((tokens, nk), F32)],
        (meta, x, *weights, *gains, *tables),
        40,
    )


def stack_heads(ref, group):
    return jnp.concatenate([ref[:, h * HEAD : (h + 1) * HEAD] for h in range(group)], axis=0)


def bounds(meta, at, row, docs, span, group):
    place = meta[at] + lax.broadcasted_iota(I32, (span, 1), 0)
    begin = jnp.zeros_like(place)
    for d in range(docs):
        start = meta[at + 1 + row * docs + d]
        begin = jnp.where(place >= start, start, begin)
    return jnp.concatenate([place] * group, axis=0), jnp.concatenate([begin] * group, axis=0)


def attend_kernel(slot_count, docs, group, scale, meta, *refs):
    q_ref, refs = refs[0], refs[1:]
    keys, refs = refs[:slot_count], refs[slot_count:]
    wo = refs[0]
    o_out, lse_out, part_out = refs[1:4]
    scores, acc = refs[4:]
    r, g, last = pl.program_id(0), pl.program_id(1), pl.num_programs(1) - 1
    first = r * slot_count
    bases = pl.num_programs(0) * slot_count
    span = q_ref.shape[0]
    queries = stack_heads(q_ref, group)
    high, low = bounds(meta, bases + slot_count + 1, r, docs, span, group)
    k_place = lax.broadcasted_iota(I32, (1, span), 1)
    top = jnp.full((group * span, HEAD), MASKED, F32)

    for s in range(slot_count):

        def some(top, s=s):
            raw = dot_nt(queries, keys[s][0, 0]) * scale
            place = k_place + meta[bases + s]
            kept = jnp.where((place >= low) & (place <= high), raw, MASKED)
            scores[s] = kept
            for c in range(span // HEAD):
                top = jnp.maximum(top, kept[:, c * HEAD : (c + 1) * HEAD])
            return top

        top = lax.cond(meta[first + s] > 0, some, lambda t: t, top)

    peak = jnp.max(top, axis=-1, keepdims=True)
    total = jnp.zeros((group * span, HEAD), F32)
    out = jnp.zeros((group * span, HEAD), F32)
    for s in range(slot_count):

        def more(carry, s=s):
            total, out = carry
            power = jnp.exp2(scores[s] - peak)
            for c in range(span // HEAD):
                total = total + power[:, c * HEAD : (c + 1) * HEAD]
            return total, out + dot_nn(power.astype(BF), keys[s][0, 1])

        total, out = lax.cond(meta[first + s] > 0, more, lambda t: t, (total, out))

    total = jnp.sum(total, axis=-1, keepdims=True)
    lse_out[0, 0] = peak + jnp.log2(total)
    out = (out / total).astype(BF)
    out = jnp.concatenate([out[h * span : (h + 1) * span] for h in range(group)], axis=1)
    o_out[...] = out
    part = dot_nn(out, wo[...])

    @pl.when(g == 0)
    def _():
        acc[...] = part

    @pl.when(g > 0)
    def _():
        acc[...] += part

    @pl.when(g == last)
    def _():
        part_out[...] = acc[...].astype(BF)


def attend_call(meta, docs, queries, kv_slots, wo):
    slot_count = len(kv_slots)
    tokens, nq = queries.shape
    row_count, _, span, nk = kv_slots[0].shape
    heads, group = nk // HEAD, nq // nk
    width = wo.shape[1]
    wide = group * HEAD
    rows = pl.BlockSpec((span, wide), lambda r, g, *_: (r, g))
    return call(
        functools.partial(attend_kernel, slot_count, docs, group, HEAD**-0.5 * LOG2E),
        (row_count, heads),
        [rows]
        + [pl.BlockSpec((1, 2, span, HEAD), lambda r, g, *_: (r, 0, 0, g))] * slot_count
        + [pl.BlockSpec((wide, width), lambda r, g, *_: (g, 0))],
        [
            rows,
            pl.BlockSpec((1, 1, group * span, 1), lambda r, g, *_: (r, g, 0, 0)),
            pl.BlockSpec((span, width), lambda r, g, *_: (r, 0)),
        ],
        [hbm((tokens, nq), BF), hbm((row_count, heads, group * span, 1), F32), hbm((tokens, width), BF)],
        [pltpu.VMEM((slot_count, group * span, span), F32), pltpu.VMEM((span, width), F32)],
        (meta, queries, *kv_slots, wo),
        40,
    )


def ff_kernel(meta, x, og, wg, wu, wd, out, keep, send):
    @pl.when(pl.program_id(0) == 0)
    def _():
        half_out(x, meta[0], keep, send)

    gate = dot_nn(x[...], wg[...])
    up = dot_nn(x[...], wu[...])
    upstream = dot_nt(og[...], wd[...])
    sigmoid = 1.0 / (1.0 + jnp.exp(-gate))
    silu = gate * sigmoid
    out[0] = (silu * up).astype(BF)
    out[1] = (upstream * up * sigmoid * (1.0 + gate * (1.0 - sigmoid))).astype(BF)
    out[2] = (upstream * silu).astype(BF)


def ff_call(meta, x, og, wg, wu, wd, after):
    tokens, width = x.shape
    hidden = wg.shape[1]
    block = 256
    column = pl.BlockSpec((width, block), lambda j, *_: (0, j))
    return call(
        ff_kernel,
        (hidden // block,),
        [whole((tokens, width))] * 2 + [column, column, pl.BlockSpec((block, width), lambda j, *_: (j, 0))],
        [pl.BlockSpec((3, tokens, block), lambda j, *_: (0, 0, j))] + [whole((tokens, width // 2))] * 2,
        [hbm((3, tokens, hidden), BF)] + [hbm((tokens, width // 2), BF)] * 2,
        [],
        (meta, x, og, wg, wu, wd),
        48,
        after=after,
    )


def ff_back_kernel(gate, up, wg, wu, out):
    out[...] = (dot_nt(gate[0], wg[...]) + dot_nt(up[0], wu[...])).astype(BF)


def ff_back_call(planes, wg, wu):
    _, tokens, hidden = planes.shape
    width = wg.shape[0]
    block = 512
    row = pl.BlockSpec((block, hidden), lambda j: (j, 0))
    plane = lambda n: pl.BlockSpec((1, tokens, hidden), lambda j: (n, 0, 0))
    return call(
        ff_back_kernel,
        (width // block,),
        [plane(1), plane(2), row, row],
        [pl.BlockSpec((tokens, block), lambda j: (0, j))],
        [hbm((tokens, width), BF)],
        [],
        (planes, planes, wg, wu),
        40,
        prefetch=0,
    )[0]


def ff_out_kernel(hm, wd, out):
    out[...] = dot_nn(hm[0], wd[...]).astype(BF)


def ff_out_call(planes, wd):
    _, tokens, hidden = planes.shape
    width = wd.shape[1]
    block = 512
    return call(
        ff_out_kernel,
        (width // block,),
        [pl.BlockSpec((1, tokens, hidden), lambda j: (0, 0, 0)), pl.BlockSpec((hidden, block), lambda j: (0, j))],
        [pl.BlockSpec((tokens, block), lambda j: (0, j))],
        [hbm((tokens, width), BF)],
        [],
        (planes, wd),
        32,
        prefetch=0,
    )[0]


def norm_back(turned, raw, gain, cos, sin):
    upstream = turned * cos - pltpu.roll(turned, HEAD // 2, 1) * sin
    inverse = lax.rsqrt(jnp.mean(raw * raw, axis=-1, keepdims=True) + EPS)
    scaled = upstream * gain
    through = inverse * scaled - raw * (inverse * inverse * inverse) * jnp.mean(
        raw * scaled, axis=-1, keepdims=True
    )
    return through.astype(BF), jnp.sum(upstream * raw * inverse, axis=0, keepdims=True)


def attend_back_kernel(slot_count, docs, group, scale, meta, *refs):
    bg, wo, q_ref, refs = refs[0], refs[1], refs[2], refs[3:]
    keys, refs = refs[:slot_count], refs[slot_count:]
    o_ref, lse_ref, q_raw, gq, cos, sin = refs[:6]
    dq_out, even_out, odd_low, odd_high, gain_out, keep, send = refs[6:]
    r, g = pl.program_id(0), pl.program_id(1)
    first = r * slot_count
    bases = pl.num_programs(0) * slot_count

    @pl.when(g == 0)
    def _():
        half_out(bg, meta[bases + slot_count], keep, send)

    @pl.when((r == 0) & (g == 0))
    def _():
        gain_out[...] = jnp.zeros_like(gain_out)

    span = q_ref.shape[0]
    d_out = dot_nt(bg[...], wo[...]).astype(BF)
    d_out = jnp.concatenate([d_out[:, h * HEAD : (h + 1) * HEAD] for h in range(group)], axis=0)
    o_rows = stack_heads(o_ref, group)
    queries = stack_heads(q_ref, group)
    centre = jnp.sum(d_out.astype(F32) * o_rows.astype(F32), axis=-1, keepdims=True)
    lse = lse_ref[0, 0]
    high, low = bounds(meta, bases + slot_count + 1, r, docs, span, group)
    k_place = lax.broadcasted_iota(I32, (1, span), 1)
    dq = jnp.zeros((group * span, HEAD), F32)
    for s in range(slot_count):
        half = slot_count // 4
        if s % 2 == 0:
            out = even_out.at[s // 2, 0]
        else:
            out = (odd_low if s // 2 < half else odd_high).at[s // 2 % half, 0]

        def some(dq, s=s, out=out):
            raw = dot_nt(queries, keys[s][0, 0]) * (scale * LOG2E)
            place = k_place + meta[bases + s]
            probs = jnp.where((place >= low) & (place <= high), jnp.exp2(raw - lse), 0.0)
            d_probs = dot_nt(d_out, keys[s][0, 1])
            d_score = (probs * (d_probs - centre)).astype(BF)
            out[0] = (dot_tn(d_score, queries) * scale).astype(BF)
            out[1] = dot_tn(probs.astype(BF), d_out).astype(BF)
            return dq + dot_nn(d_score, keys[s][0, 0])

        def none(dq, out=out):
            out[...] = jnp.zeros(out.shape, BF)
            return dq

        dq = lax.cond(meta[first + s] > 0, some, none, dq)

    gain = gq[...]
    gain_total = jnp.zeros((1, HEAD), F32)
    for h in range(group):
        rows = dq[h * span : (h + 1) * span] * scale
        d_raw, part = norm_back(rows, q_raw[:, h * HEAD : (h + 1) * HEAD], gain, cos[...], sin[...])
        dq_out[:, h * HEAD : (h + 1) * HEAD] = d_raw
        gain_total = gain_total + part
    gain_out[...] += gain_total


def attend_back_call(meta, docs, bg, wo, queries, kv_slots, attended, lse, q_raw, gq, tables, after):
    slot_count = len(kv_slots)
    tokens, width = bg.shape
    nq = queries.shape[1]
    row_count, _, span, nk = kv_slots[0].shape
    heads, group = nk // HEAD, nq // nk
    wide = group * HEAD
    rows = pl.BlockSpec((span, wide), lambda r, g, *_: (r, g))
    by_row = lambda n: pl.BlockSpec((span, n), lambda r, g, *_: (r, 0))
    kv_out = lambda n: pl.BlockSpec((n, 1, 2, span, HEAD), lambda r, g, *_: (0, r, 0, 0, g))
    kv_shape = lambda n: hbm((n, row_count, 2, span, nk), BF)
    half, quarter = slot_count // 2, slot_count // 4
    return call(
        functools.partial(attend_back_kernel, slot_count, docs, group, HEAD**-0.5),
        (row_count, heads),
        [by_row(width), pl.BlockSpec((wide, width), lambda r, g, *_: (g, 0)), rows]
        + [pl.BlockSpec((1, 2, span, HEAD), lambda r, g, *_: (r, 0, 0, g))] * slot_count
        + [rows, pl.BlockSpec((1, 1, group * span, 1), lambda r, g, *_: (r, g, 0, 0))]
        + [rows, whole((1, HEAD)), by_row(HEAD), by_row(HEAD)],
        [rows, kv_out(half), kv_out(quarter), kv_out(quarter), whole((1, HEAD)), by_row(width // 2), by_row(width // 2)],
        [
            hbm((tokens, nq), BF),
            kv_shape(half),
            kv_shape(quarter),
            kv_shape(quarter),
            sds((1, HEAD), F32),
            hbm((tokens, width // 2), BF),
            hbm((tokens, width // 2), BF),
        ],
        [],
        (meta, bg, wo, queries, *kv_slots, attended, lse, q_raw, gq, *tables),
        40,
        after=after,
    )


def key_back_kernel(count, row_count, *refs):
    pieces, refs = refs[:count], refs[count:]
    dq_ref, k_raw, gk, cos, sin, all_out, gain_out = refs
    span, nk = pieces[0].shape[2:]
    nq = dq_ref.shape[1]
    all_out[:, :nq] = dq_ref[...]
    gain_total = jnp.zeros((1, HEAD), F32)
    for r in range(row_count):
        rows = slice(r * span, (r + 1) * span)
        for h in range(nk // HEAD):
            at = slice(h * HEAD, (h + 1) * HEAD)
            turned = sum(p[r, 0, :, at].astype(F32) for p in pieces)
            d_raw, part = norm_back(turned, k_raw[rows, at], gk[...], cos[rows], sin[rows])
            all_out[rows, nq + h * HEAD : nq + (h + 1) * HEAD] = d_raw
            gain_total = gain_total + part
        all_out[rows, nq + nk :] = sum(p[r, 1].astype(F32) for p in pieces).astype(BF)
    gain_out[...] = gain_total


def key_back_call(pieces, dq, k_raw, gk, tables, after):
    tokens, nq = dq.shape
    nk = k_raw.shape[1]
    return call(
        functools.partial(key_back_kernel, len(pieces), pieces[0].shape[0]),
        (1,),
        [whole(pieces[0].shape)] * len(pieces)
        + [whole((tokens, nq)), whole((tokens, nk)), whole((1, HEAD)), whole((tokens, HEAD)), whole((tokens, HEAD))],
        [whole((tokens, nq + 2 * nk)), whole((1, HEAD))],
        [hbm((tokens, nq + 2 * nk), BF), hbm((1, HEAD), F32)],
        [],
        (*pieces, dq, k_raw, gk, *tables),
        40,
        prefetch=0,
        after=after,
    )


def back_kernel(grads, wq, wk, wv, out):
    nq, nk = wq.shape[1], wk.shape[1]
    part = (
        dot_nt(grads[:, :nq], wq[...])
        + dot_nt(grads[:, nq : nq + nk], wk[...])
        + dot_nt(grads[:, nq + nk :], wv[...])
    )
    out[...] = part.astype(BF)


def back_call(grads, weights):
    tokens, cols = grads.shape
    width = weights[0].shape[0]
    block = width // 4
    return call(
        back_kernel,
        (4,),
        [whole((tokens, cols))] + [pl.BlockSpec((block, w.shape[1]), lambda j: (j, 0)) for w in weights],
        [pl.BlockSpec((tokens, block), lambda j: (0, j))],
        [hbm((tokens, width), BF)],
        [],
        (grads, *weights),
        40,
        prefetch=0,
    )[0]


def turn_rows(ids, parts, left_refs, turned):
    tokens, rows = left_refs[0].shape
    part = turned.shape[0] // parts
    for k, ref in enumerate(left_refs):
        for n in range(parts):
            block = ref[:, pl.ds(pl.multiple_of(ids[n] * part, HEAD), part)]
            turned[n * part : (n + 1) * part, k * tokens : (k + 1) * tokens] = block.T


def put_rows(total, outs, at):
    part = total.shape[0] // len(outs)
    for n, out in enumerate(outs):
        out[at] = total[n * part : (n + 1) * part].astype(BF)


def ff_grad_kernel(ids, og0, og1, x0, x1, p0, p1, *refs):
    outs, turned = refs[:-1], refs[-1]

    @pl.when(pl.program_id(0) == 0)
    def _():
        turn_rows(ids, len(outs), (og0, og1), turned.at[0])
        turn_rows(ids, len(outs), (x0, x1), turned.at[1])

    for n in range(3):
        right = jnp.concatenate([p0[n], p1[n]], axis=0)
        put_rows(dot_nn(turned[min(n, 1)], right), outs, n)


def ff_grad_call(ids, ogs, xs, planes):
    tokens, rows = xs[0].shape
    hidden = planes[0].shape[2]
    wide = next(w for w in (512, 384, 256, 128) if hidden % w == 0)
    part = rows // 4
    count = ids.shape[0]
    return call(
        ff_grad_kernel,
        (hidden // wide,),
        [whole((tokens, rows))] * 4 + [pl.BlockSpec((3, tokens, wide), lambda c, ids: (0, 0, c))] * 2,
        [pl.BlockSpec((3, part, wide), lambda c, ids: (0, 0, c))] * count,
        [hbm((3, part, hidden), BF)] * count,
        [pltpu.VMEM((2, count * part, 2 * tokens), BF)],
        (ids, *ogs, *xs, *planes),
        48,
        free=True,
    )


def attn_grad_kernel(steps, ids, x0, x1, b0, b1, g0, g1, o0, o1, *refs):
    outs, turned = refs[:-1], refs[-1]
    c = pl.program_id(0)

    @pl.when(c == 0)
    def _():
        turn_rows(ids, len(outs), (x0, x1), turned)

    @pl.when(c == steps)
    def _():
        turn_rows(ids, len(outs), (b0, b1), turned)

    @pl.when(c < steps)
    def _():
        put_rows(dot_nn(turned[...], jnp.concatenate([g0[...], g1[...]], axis=0)), outs, 0)

    @pl.when(c >= steps)
    def _():
        put_rows(dot_nn(turned[...], jnp.concatenate([o0[...], o1[...]], axis=0)), outs, 0)


def attn_grad_call(ids, xs, bs, grads, outs):
    tokens, rows = xs[0].shape
    wide = outs[0].shape[1] if grads[0].shape[1] % outs[0].shape[1] == 0 else HEAD
    steps = grads[0].shape[1] // wide
    more = outs[0].shape[1] // wide
    part = rows // 4
    count = ids.shape[0]
    cols = (steps + more) * wide
    return call(
        functools.partial(attn_grad_kernel, steps),
        (steps + more,),
        [whole((tokens, rows))] * 4
        + [pl.BlockSpec((tokens, wide), lambda c, ids: (0, jnp.minimum(c, steps - 1)))] * 2
        + [pl.BlockSpec((tokens, wide), lambda c, ids: (0, jnp.maximum(c - steps, 0)))] * 2,
        [pl.BlockSpec((1, part, wide), lambda c, ids: (0, 0, c))] * count,
        [hbm((1, part, cols), BF)] * count,
        [pltpu.VMEM((count * part, 2 * tokens), BF)],
        (ids, *xs, *bs, *grads, *outs),
        48,
    )


def split_kernel(bits, keep_a, got_a, keep_b, got_b, send_a, next_a, send_b, next_b):
    j = pl.program_id(0)

    def put(out, keep, got):
        out[...] = (keep[...].astype(F32) + got[...].astype(F32)).astype(BF)

    @pl.when(j == 0)
    def _():
        put(send_a, keep_a, got_a)
        put(send_b, keep_b, got_b)

    @pl.when(j == 1)
    def _():
        put(next_a, keep_a, got_a)
        put(next_b, keep_b, got_b)


def split_call(bits, keeps, gots, after):
    *lead, rows, cols = keeps[0].shape
    zeros = (0,) * len(lead)
    half = (*lead, rows // 2, cols)
    part = lambda f: pl.BlockSpec(half, lambda j, bits: (*zeros, jnp.where(j == 0, 1 - bits[f], bits[f]), 0))
    send_a, next_a, send_b, next_b = call(
        split_kernel,
        (2,),
        [part(0), part(0), part(1), part(1)],
        [whole(half)] * 4,
        [hbm(half, BF)] * 4,
        [],
        (bits, keeps[0], gots[0], keeps[1], gots[1]),
        40,
        after=after,
    )
    return (send_a, send_b), (next_a, next_b)


def sum_kernel(bits, *refs):
    count = (len(refs) - 2) // 2
    for f, out in enumerate(refs[2 * count :]):
        total = refs[f * count][...].astype(F32)
        for ref in refs[f * count + 1 : (f + 1) * count]:
            total = total + ref[...].astype(F32)
        out[...] = total.astype(BF)


def sum_call(bits, flows, after=()):
    rows = min(v.shape[1] for v in flows[0])
    planes, _, cols = flows[0][0].shape
    block = (planes, rows // 2, cols)

    def part(v, f):
        long = v.shape[1] > rows
        return pl.BlockSpec(block, lambda j, bits: (0, j + (2 * bits[f] if long else 0), 0))

    return call(
        sum_kernel,
        (2,),
        [part(v, f) for f, vs in enumerate(flows) for v in vs],
        [pl.BlockSpec(block, lambda j, bits: (0, j, 0))] * 2,
        [hbm((planes, rows, cols), BF)] * 2,
        [],
        (bits, *(v for f in flows for v in (*(in_hbm(k) for k in f[:-1]), f[-1]))),
        40,
        after=after,
        free=True,
    )


def half_sum_call(bits, keeps, gots):
    planes, rows, cols = keeps[0].shape
    block = (planes, rows // 4, cols)
    part = lambda f: pl.BlockSpec(block, lambda j, bits: (0, j + 2 * bits[f], 0))
    return call(
        sum_kernel,
        (2,),
        [part(0), part(0), part(1), part(1)],
        [pl.BlockSpec(block, lambda j, bits: (0, j, 0))] * 2,
        [hbm((planes, rows // 2, cols), BF)] * 2,
        [],
        (bits, keeps[0], gots[0], keeps[1], gots[1]),
        40,
        free=planes == 1,
    )


def widen_kernel(count, size, planes, turned, onto, table, *refs):
    pieces, outs = refs[: count * size * planes], refs[count * size * planes + onto :]

    def put(refs, at_row):
        rows = refs[0].shape[1]
        at_row = slice(None) if size == 1 else pl.ds(pl.multiple_of(at_row * rows, rows), rows)
        at, plane = 0, 0
        for k, out in enumerate(outs):
            wide = out.shape[0 if k in turned else 1]
            value = refs[plane][0, :, at : at + wide]
            if k in turned:
                out[:, at_row] = value.T.astype(F32)
            else:
                out[at_row, :] = value.astype(F32)
            at += wide
            if at == refs[plane].shape[2]:
                at, plane = 0, plane + 1

    for k in range(count):

        @pl.when(pl.program_id(0) == k)
        def _(k=k):
            for n in range(k * size, (k + 1) * size):
                put(pieces[n * planes : (n + 1) * planes], table[count + n])


def widen_call(blocks, spots, groups, planes, shapes, turned, onto, after):
    count, size = len(groups), len(groups[0])
    _, rows, cols = groups[0][0].shape
    place = lambda n: pl.BlockSpec((1, rows, cols), lambda j, t: (n, 0, 0), pipeline_mode=pl.Buffered(1))
    by_row = lambda s: pl.BlockSpec((size * rows, s[1]), lambda j, t: (t[j], 0))
    by_col = lambda s: pl.BlockSpec((s[0], size * rows), lambda j, t: (0, t[j]))
    return call(
        functools.partial(widen_kernel, count, size, len(planes), turned, len(onto)),
        (count,),
        [place(n) for _ in range(count * size) for n in planes] + [pl.BlockSpec(memory_space=pl.ANY)] * len(onto),
        [by_col(s) if k in turned else by_row(s) for k, s in enumerate(shapes)],
        [hbm(s, F32) for s in shapes],
        [],
        (jnp.concatenate([blocks, spots]), *(p for g in groups for p in g for _ in planes), *onto),
        56,
        after=after,
        free=True,
        aliases={1 + count * size * len(planes) + k: k for k in range(len(onto))},
    )


def hold_kernel(a, b, a_out, b_out):
    a_out[...] = a[...]
    b_out[...] = b[...]


def hold_call(values):
    planes, rows, cols = values[0].shape
    block = pl.BlockSpec((1, rows, cols), lambda j: (j, 0, 0))
    return call(
        hold_kernel,
        (planes,),
        [block] * 2,
        [block] * 2,
        [hbm(values[0].shape, BF)] * 2,
        [],
        tuple(values),
        24,
        prefetch=0,
    )


def norm_kernel(x, gain, out):
    value = x[...].astype(F32)
    inverse = lax.rsqrt(jnp.mean(value * value, axis=-1, keepdims=True) + EPS)
    out[...] = (value * inverse * gain[...]).astype(BF)


def norm_call(x, gain):
    return call(
        norm_kernel,
        (1,),
        [whole(x.shape), whole(gain.shape)],
        [whole(x.shape)],
        [hbm(x.shape, BF)],
        [],
        (x, gain),
        24,
        prefetch=0,
    )[0]


def middle_kernel(x, got, gain, middle, out):
    value = x[...].astype(F32) + got[...].astype(F32)
    inverse = lax.rsqrt(jnp.mean(value * value, axis=-1, keepdims=True) + EPS)
    middle[...] = value
    out[...] = (value * inverse * gain[...]).astype(BF)


def middle_call(x, got, gain, after):
    return call(
        middle_kernel,
        (1,),
        [whole(x.shape), whole(x.shape), whole(gain.shape)],
        [whole(x.shape)] * 2,
        [hbm(x.shape, F32), hbm(x.shape, BF)],
        [],
        (x, got, gain),
        24,
        prefetch=0,
        after=after,
    )


def norm_grad_kernel(x, got, base, gain, *outs):
    value, upstream = x[...].astype(F32), got[...].astype(F32)
    inverse = lax.rsqrt(jnp.mean(value * value, axis=-1, keepdims=True) + EPS)
    scaled = upstream * gain[...]
    through = inverse * scaled - value * (inverse * inverse * inverse) * jnp.mean(
        value * scaled, axis=-1, keepdims=True
    )
    total = base[...].astype(F32) + through
    outs[0][...] = total
    outs[1][...] = jnp.sum(upstream * value * inverse, axis=0, keepdims=True)
    if len(outs) > 2:
        outs[2][...] = total.astype(BF)


def norm_grad_call(x, got, base, gain, low, after=()):
    return call(
        norm_grad_kernel,
        (1,),
        [whole(x.shape)] * 3 + [whole(gain.shape)],
        [whole(x.shape), whole(gain.shape)] + [whole(x.shape)] * low,
        [hbm(x.shape, F32), hbm(gain.shape, F32)] + [hbm(x.shape, BF)] * low,
        [],
        (x, got, base, gain),
        24,
        prefetch=0,
        after=after,
    )


class WeightSum:
    def __init__(self, masks):
        self.flows = (masks, masks[::-1])
        seq = lax.axis_index("seq")
        self.core = seq & 1
        self.bits = [jnp.stack([(seq & m[k]) // m[k] for m in self.flows]) for k in range(len(masks))]
        base = jnp.array([0, 2], I32)
        self.send_ids, self.keep_ids = base + 1 - self.bits[0], base + self.bits[0]
        self.level = 0

    def swap_level(self, sends):
        self.gots = [swap(s, "seq", m[self.level]) for s, m in zip(sends, self.flows)]
        self.level += 1

    def begin(self, sends):
        self.swap_level(sends)

    def middle(self):
        count = len(self.flows[0])
        self.terms = [[k] for k in self.kept]
        while self.level < count:
            bits = self.bits[self.level]
            if self.level < count - 1:
                sends, kept = split_call(bits, self.kept, self.gots, ())
                self.kept = kept
            else:
                sends = half_sum_call(1 - bits, self.kept, self.gots)
                self.terms = [[k, g] for k, g in zip(self.kept, self.gots)]
            self.swap_level(sends)
        self.terms = [t + [g] for t, g in zip(self.terms, self.gots)]

    def last(self, after=()):
        parts = sum_call(self.bits[-1], self.terms, after)
        for level in range(len(self.flows[0]) - 1, 0, -1):
            gots = [swap(p, "seq", m[level]) for p, m in zip(parts, self.flows)]
            parts = [
                jnp.where(self.bits[level][f] == 0, *(jnp.concatenate(v, axis=1) for v in ((p, g), (g, p))))
                for f, (p, g) in enumerate(zip(parts, gots))
            ]
        self.parts, self.spots = parts, jnp.zeros((8,), I32)
        ends = [v for p, m in zip(parts, self.flows) for v in (p, swap(p, "seq", m[0]))]
        self.groups = [(v,) for v in (*ends, *(self.other(v) for v in ends))]
        self.soon = ends

    def other(self, value):
        return swap(value, "seq", 1)

    def last_in_pieces(self):
        self.own = sum_call(self.bits[-1], self.terms)
        self.near = [swap(p, "seq", m[1]) for p, m in zip(self.own, self.flows)]
        self.parts = [self.other(v) for v in (*self.own, *self.near)]
        self.far = [swap(p, "seq", m[0]) for p, m in zip(self.own, self.flows)]
        self.soon = [self.other(v) for v in self.far]

    def finish(self):
        last = [swap(p, "seq", m[0]) for p, m in zip(hold_call(self.near), self.flows)]
        own, other = [], []
        for f in range(2):
            own += [(self.own[f], self.near[f]), (self.far[f], last[f])]
            other += [(self.parts[f], self.parts[2 + f]), (self.soon[f], self.other(last[f]))]
        self.groups = own + other
        spots = jnp.stack([s for b in self.bits[1] for s in (b, 1 - b, b, 1 - b)])
        self.spots = jnp.concatenate([spots, spots])

    def widen(self, planes, shapes, turned, early=False, onto=(), after=()):
        blocks = jnp.stack([h for f in range(2) for h in (2 * f + self.bits[0][f], 2 * f + 1 - self.bits[0][f])])
        table = jnp.concatenate([self.core * 4 + blocks, (1 - self.core) * 4 + blocks])
        half = slice(None) if not early and not onto else slice(0 if early else 1, None, 2)
        spots = self.spots.reshape(8, -1)[half].reshape(-1)
        return widen_call(table[half], spots, self.groups[half], planes, shapes, turned, tuple(onto), after)


def halves(value, core):
    half = value.shape[1] // 2
    return (
        lax.dynamic_slice_in_dim(value, core * half, half, 1),
        lax.dynamic_slice_in_dim(value, (1 - core) * half, half, 1),
    )


def body(
    hidden_in,
    output_grad,
    document_lengths,
    attention_gain,
    query_weight,
    key_weight,
    value_weight,
    query_gain,
    key_gain,
    output_weight,
    feedforward_gain,
    gate_weight,
    up_weight,
    down_weight,
):
    ORDER.clear()
    tp, seqs = lax.axis_size("tp"), lax.axis_size("seq")
    seq_at = lax.axis_index("seq")
    core = seq_at & 1
    row_count, share, width = hidden_in.shape
    span = share * tp
    masks = tuple(1 << b for b in range(1, seqs.bit_length() - 1))

    ends = jnp.stack(
        [jnp.sum(document_lengths[:, : n + 1], axis=1) for n in range(document_lengths.shape[1])], axis=1
    )
    starts = ends - document_lengths
    docs = document_lengths.shape[1]
    places = seq_at * span + jnp.arange(span, dtype=I32)
    inside = (places[None, :, None] >= starts[:, None]) & (places[None, :, None] < ends[:, None])
    begun = jnp.sum(jnp.where(inside, starts[:, None], 0), axis=2)
    slot_seq = jnp.arange(seqs, dtype=I32) ^ seq_at
    needed = (slot_seq <= seq_at)[None] & ((slot_seq + 1)[None] * span > begun[:, :1])
    meta = jnp.concatenate(
        [needed.astype(I32).reshape(-1), slot_seq * span, core[None], places[:1], starts.reshape(-1)]
    )
    frequency = ROPE_BASE ** (-2.0 * jnp.arange(HEAD // 2, dtype=F32) / HEAD)
    angles = (places[None] - begun).reshape(-1, 1).astype(F32) * frequency
    cos, sin = jnp.cos(angles), jnp.sin(angles)
    tables = (jnp.concatenate([cos, cos], 1), jnp.concatenate([-sin, sin], 1))
    core_meta = core[None]
    q_gain, k_gain = query_gain[None], key_gain[None]
    qkv_weights = (query_weight, key_weight, value_weight)

    flat = lambda v: v.reshape(-1, width)
    hidden, upward = flat(hidden_in), flat(output_grad)
    attn_gain, ff_gain = attention_gain[None], feedforward_gain[None]
    shares = lambda v: v.reshape(row_count, share, width)
    normed1 = gather_tp(shares(norm_call(hidden, attn_gain)))
    queries, kv, q_raw, k_raw, n1_keep, n1_send = qkv_call(
        core_meta, row_count, normed1, qkv_weights, (q_gain, k_gain), tables
    )
    grads = gather_tp(output_grad)
    kv_slots = []
    for value in [kv] + [swap(kv, "seq", m) for m in range(2, seqs, 2)]:
        kv_slots += [value, swap(value, "seq", 1)]
    attended, lse, o_part = attend_call(meta, docs, queries, kv_slots, output_weight)

    def both(own, sent=None):
        return [own, swap(own if sent is None else sent, "seq", 1)]

    o_both = both(attended)
    n1_both = both(n1_keep, n1_send)
    middle, normed2 = middle_call(hidden, flat(scatter_tp(o_part, row_count)), ff_gain, (grads,))
    grads_both = both(*halves(grads, core))
    normed2 = gather_tp(shares(normed2))
    planes, n2_keep, n2_send = ff_call(
        core_meta, normed2, grads, gate_weight, up_weight, down_weight, (grads_both[1], o_both[1], n1_both[1])
    )
    planes_both, n2_both = both(planes), both(n2_keep, n2_send)
    n2_got = scatter_tp(ff_back_call(planes, gate_weight, up_weight), row_count)

    ff = WeightSum(masks)
    ff.begin(ff_grad_call(ff.send_ids, grads_both, n2_both, planes_both))
    ff.kept = ff_grad_call(ff.keep_ids, grads_both, n2_both, planes_both)
    middle_grad, ff_gain_grad, branch = norm_grad_call(middle, flat(n2_got), upward, ff_gain, True, ff.gots)
    branch = gather_tp(shares(branch))
    ff.middle()
    ff_got = scatter_tp(ff_out_call(planes, down_weight), row_count)
    in_pieces = len(masks) == 2
    if in_pieces:
        ff.last_in_pieces()
    else:
        ff.last()
    dq, even, odd_low, odd_high, q_gain_grad, b_keep, b_send = attend_back_call(
        meta,
        docs,
        branch,
        output_weight,
        queries,
        kv_slots,
        attended,
        lse,
        q_raw,
        q_gain,
        tables,
        ff.parts,
    )
    odd = [v[k] for v in (swap(odd_low, "seq", 1), swap(odd_high, "seq", 1)) for k in range(seqs // 4)]
    chip = [(even[k].astype(F32) + odd[k].astype(F32)).astype(BF) for k in range(seqs // 2)]
    pieces = [chip[0]] + [swap(chip[m // 2], "seq", m) for m in range(2, seqs, 2)]
    bg_both = both(b_keep, b_send)
    all_grad, k_gain_grad = key_back_call(pieces, dq, k_raw, k_gain, tables, (*ff.soon, ff_got, bg_both[1]))
    all_both = both(all_grad)
    n1_got = scatter_tp(back_call(all_grad, qkv_weights), row_count)
    if in_pieces:
        ff.finish()
    attn = WeightSum(masks)
    ids = jnp.concatenate([attn.send_ids, attn.keep_ids])
    parts = attn_grad_call(ids, n1_both, bg_both, all_both, o_both)
    attn.kept = parts[2:]
    attn.begin(parts[:2])
    gate_up = ((1, 2), [gate_weight.shape, up_weight.shape], ())
    down = ((0,), [down_weight.shape], (0,))
    attend = ((0,), [w.shape for w in (*qkv_weights, output_weight)], (3,))
    gate_up_out, down_out = ff.widen(*gate_up, early=True), ff.widen(*down, early=True)
    attn.middle()
    input_grad, attn_gain_grad = norm_grad_call(hidden, flat(n1_got), middle_grad, attn_gain, False)
    gains = jnp.concatenate(
        [v.reshape(-1) for v in (attn_gain_grad, ff_gain_grad, q_gain_grad, k_gain_grad)]
    ).reshape(-1, HEAD)
    gains = sum_copies(gains, "tp", [1 << level for level in range(tp.bit_length() - 1)])
    for level in range(seqs.bit_length() - 1):
        gains = sum_copies(gains, "seq", [1 << level])
    input_grad = shares(input_grad)
    block_out = shares((middle + flat(ff_got).astype(F32)).astype(BF))
    gate_out, up_out = ff.widen(*gate_up, onto=gate_up_out)
    attn.last()
    (down_out,) = ff.widen(*down, onto=down_out)
    query_out, key_out, value_out, output_out = attn.widen(*attend)
    gains = gains.reshape(-1)
    return (
        block_out,
        input_grad,
        gains[:width],
        query_out,
        key_out,
        value_out,
        gains[2 * width : 2 * width + HEAD],
        gains[2 * width + HEAD :],
        output_out,
        gains[width : 2 * width],
        gate_out,
        up_out,
        down_out,
    )


def solution(mesh):
    tokens, columns, rows = P(None, ("seq", "tp"), None), P(None, "tp"), P("tp", None)
    in_specs = (
        tokens,
        tokens,
        P(),
        P(),
        columns,
        columns,
        columns,
        P(),
        P(),
        rows,
        P(),
        columns,
        columns,
        rows,
    )
    out_specs = (
        tokens,
        tokens,
        P(),
        columns,
        columns,
        columns,
        P(),
        P(),
        rows,
        P(),
        columns,
        columns,
        rows,
    )
    return jax.shard_map(body, mesh=mesh, in_specs=in_specs, out_specs=out_specs, check_vma=False)
```

```python
import functools
import math

import jax
import jax.numpy as jnp
from jax import lax
from jax.experimental import pallas as pl
from jax.experimental.pallas import tpu as pltpu
from jax.sharding import PartitionSpec as P

HEAD = 128
EPS = 1e-06
ROPE_BASE = 1000000.0
MASKED = -1e30
LOG2E = math.log2(math.e)
BF = jnp.bfloat16
F32 = jnp.float32
I32 = jnp.int32


def sds(shape, dtype):
    return jax.ShapeDtypeStruct(shape, dtype)


def hbm(shape, dtype):
    return pltpu.HBM(shape, dtype)


def whole(shape):
    return pl.BlockSpec(shape, lambda *_: (0,) * len(shape))


def dot_nn(a, b):
    return lax.dot_general(a, b, (((1,), (0,)), ((), ())), preferred_element_type=F32)


def dot_nt(a, b):
    return lax.dot_general(a, b, (((1,), (1,)), ((), ())), preferred_element_type=F32)


def dot_tn(a, b):
    return lax.dot_general(a, b, (((0,), (0,)), ((), ())), preferred_element_type=F32)


def in_hbm(value):
    return pltpu.with_memory_space_constraint(value, pltpu.HBM)


def call(body, grid, in_specs, out_specs, out_shape, scratch, operands, mib, prefetch=1, after=(), free=False, aliases={}):
    after = (*ORDER, *after)
    at, extra = prefetch + len(in_specs), len(after)

    def run(*refs):
        return body(*refs[:at], *refs[at + extra :])

    if not free:
        operands = operands[:prefetch] + tuple(in_hbm(v) for v in operands[prefetch:])
    outs = pl.pallas_call(
        run,
        grid_spec=pltpu.PrefetchScalarGridSpec(
            num_scalar_prefetch=prefetch,
            grid=grid,
            in_specs=in_specs + [pl.BlockSpec(memory_space=pl.ANY)] * extra,
            out_specs=out_specs,
            scratch_shapes=scratch,
        ),
        out_shape=out_shape,
        input_output_aliases=aliases,
        compiler_params=pltpu.CompilerParams(
            vmem_limit_bytes=mib << 20, dimension_semantics=("arbitrary",) * len(grid)
        ),
        cost_estimate=pl.CostEstimate(flops=1, bytes_accessed=1, transcendentals=0),
    )(*operands, *(in_hbm(v) for v in after))
    ORDER[:] = [outs[0]]
    return outs


ORDER = []


def flip(axis, mask):
    return [(i, i ^ mask) for i in range(lax.axis_size(axis))]


def swap(value, axis, mask):
    return lax.ppermute(value, axis, flip(axis, mask))


def sum_copies(value, axis, masks):
    while masks:
        if len(masks) % 2:
            value = value + swap(value, axis, masks[0])
            masks = masks[1:]
        else:
            a, b = masks[:2]
            value = (value + swap(value, axis, a)) + (swap(value, axis, b) + swap(value, axis, a | b))
            masks = masks[2:]
    return value


def gather_tp(share):
    rows, _, width = share.shape
    return lax.all_gather(share, "tp", axis=1, tiled=True).reshape(-1, width)


def scatter_tp(part, row_count):
    part = part.reshape(row_count, -1, part.shape[1])
    return lax.psum_scatter(part, "tp", scatter_dimension=1, tiled=True)


def half_out(x_ref, core, keep_ref, send_ref):
    half = keep_ref.shape[1]
    keep_ref[...] = x_ref[:, pl.ds(pl.multiple_of(core * half, half), half)]
    send_ref[...] = x_ref[:, pl.ds(pl.multiple_of((1 - core) * half, half), half)]


def qkv_kernel(row_count, meta, x, wq, wk, wv, gq, gk, cos, sin, q_out, kv_out, q_raw, k_raw, keep, send):
    @pl.when(pl.program_id(0) == 0)
    def _():
        half_out(x, meta[0], keep, send)

    def turn(raw, gain):
        inverse = lax.rsqrt(jnp.mean(raw * raw, axis=-1, keepdims=True) + EPS)
        normed = raw * inverse * gain
        return (normed * cos[...] + pltpu.roll(normed, HEAD // 2, 1) * sin[...]).astype(BF)

    query, key, value = dot_nn(x[...], wq[...]), dot_nn(x[...], wk[...]), dot_nn(x[...], wv[...])
    q_raw[...] = query
    k_raw[...] = key
    for h in range(query.shape[1] // HEAD):
        at = slice(h * HEAD, (h + 1) * HEAD)
        q_out[:, at] = turn(query[:, at], gq[...])
    turned = turn(key, gk[...])
    span = kv_out.shape[2]
    for r in range(row_count):
        kv_out[r, 0] = turned[r * span : (r + 1) * span]
        kv_out[r, 1] = value[r * span : (r + 1) * span].astype(BF)


def qkv_call(meta, row_count, x, weights, gains, tables):
    tokens, width = x.shape
    nq, nk = weights[0].shape[1], weights[1].shape[1]
    heads = nk // HEAD
    column = lambda rows, n: pl.BlockSpec((rows, n), lambda j, *_: (0, j))
    span = tokens // row_count
    return call(
        functools.partial(qkv_kernel, row_count),
        (heads,),
        [whole((tokens, width)), column(width, nq // heads), column(width, HEAD), column(width, HEAD)]
        + [whole((1, HEAD))] * 2
        + [whole((tokens, HEAD))] * 2,
        [column(tokens, nq // heads), pl.BlockSpec((row_count, 2, span, HEAD), lambda j, *_: (0, 0, 0, j))]
        + [column(tokens, nq // heads), column(tokens, HEAD)]
        + [whole((tokens, width // 2))] * 2,
        [hbm((tokens, nq), BF), hbm((row_count, 2, span, nk), BF), hbm((tokens, nq), F32), hbm((tokens, nk), F32)]
        + [hbm((tokens, width // 2), BF)] * 2,
        [],
        (meta, x, *weights, *gains, *tables),
        40,
    )


def stack_heads(ref, group):
    return jnp.concatenate([ref[:, h * HEAD : (h + 1) * HEAD] for h in range(group)], axis=0)


def bounds(meta, at, row, docs, span, group):
    place = meta[at] + lax.broadcasted_iota(I32, (span, 1), 0)
    begin = jnp.zeros_like(place)
    for d in range(docs):
        start = meta[at + 1 + row * docs + d]
        begin = jnp.where(place >= start, start, begin)
    return jnp.concatenate([place] * group, axis=0), jnp.concatenate([begin] * group, axis=0)


def attend_kernel(slot_count, docs, group, scale, meta, *refs):
    q_ref, refs = refs[0], refs[1:]
    keys, refs = refs[:slot_count], refs[slot_count:]
    wo = refs[0]
    o_out, lse_out, part_out = refs[1:4]
    scores, acc = refs[4:]
    r, g, last = pl.program_id(0), pl.program_id(1), pl.num_programs(1) - 1
    first = r * slot_count
    bases = pl.num_programs(0) * slot_count
    span = q_ref.shape[0]
    queries = stack_heads(q_ref, group)
    high, low = bounds(meta, bases + slot_count + 1, r, docs, span, group)
    k_place = lax.broadcasted_iota(I32, (1, span), 1)
    top = jnp.full((group * span, HEAD), MASKED, F32)

    for s in range(slot_count):

        def some(top, s=s):
            raw = dot_nt(queries, keys[s][0, 0]) * scale
            place = k_place + meta[bases + s]
            kept = jnp.where((place >= low) & (place <= high), raw, MASKED)
            scores[s] = kept
            for c in range(span // HEAD):
                top = jnp.maximum(top, kept[:, c * HEAD : (c + 1) * HEAD])
            return top

        top = lax.cond(meta[first + s] > 0, some, lambda t: t, top)

    peak = jnp.max(top, axis=-1, keepdims=True)
    total = jnp.zeros((group * span, HEAD), F32)
    out = jnp.zeros((group * span, HEAD), F32)
    for s in range(slot_count):

        def more(carry, s=s):
            total, out = carry
            power = jnp.exp2(scores[s] - peak)
            for c in range(span // HEAD):
                total = total + power[:, c * HEAD : (c + 1) * HEAD]
            return total, out + dot_nn(power.astype(BF), keys[s][0, 1])

        total, out = lax.cond(meta[first + s] > 0, more, lambda t: t, (total, out))

    total = jnp.sum(total, axis=-1, keepdims=True)
    lse_out[0, 0] = peak + jnp.log2(total)
    out = (out / total).astype(BF)
    out = jnp.concatenate([out[h * span : (h + 1) * span] for h in range(group)], axis=1)
    o_out[...] = out
    part = dot_nn(out, wo[...])

    @pl.when(g == 0)
    def _():
        acc[...] = part

    @pl.when(g > 0)
    def _():
        acc[...] += part

    @pl.when(g == last)
    def _():
        part_out[...] = acc[...].astype(BF)


def attend_call(meta, docs, queries, kv_slots, wo):
    slot_count = len(kv_slots)
    tokens, nq = queries.shape
    row_count, _, span, nk = kv_slots[0].shape
    heads, group = nk // HEAD, nq // nk
    width = wo.shape[1]
    wide = group * HEAD
    rows = pl.BlockSpec((span, wide), lambda r, g, *_: (r, g))
    return call(
        functools.partial(attend_kernel, slot_count, docs, group, HEAD**-0.5 * LOG2E),
        (row_count, heads),
        [rows]
        + [pl.BlockSpec((1, 2, span, HEAD), lambda r, g, *_: (r, 0, 0, g))] * slot_count
        + [pl.BlockSpec((wide, width), lambda r, g, *_: (g, 0))],
        [
            rows,
            pl.BlockSpec((1, 1, group * span, 1), lambda r, g, *_: (r, g, 0, 0)),
            pl.BlockSpec((span, width), lambda r, g, *_: (r, 0)),
        ],
        [hbm((tokens, nq), BF), hbm((row_count, heads, group * span, 1), F32), hbm((tokens, width), BF)],
        [pltpu.VMEM((slot_count, group * span, span), F32), pltpu.VMEM((span, width), F32)],
        (meta, queries, *kv_slots, wo),
        40,
    )


def ff_kernel(meta, x, og, wg, wu, wd, out, keep, send):
    @pl.when(pl.program_id(0) == 0)
    def _():
        half_out(x, meta[0], keep, send)

    gate = dot_nn(x[...], wg[...])
    up = dot_nn(x[...], wu[...])
    upstream = dot_nt(og[...], wd[...])
    sigmoid = 1.0 / (1.0 + jnp.exp(-gate))
    silu = gate * sigmoid
    out[0] = (silu * up).astype(BF)
    out[1] = (upstream * up * sigmoid * (1.0 + gate * (1.0 - sigmoid))).astype(BF)
    out[2] = (upstream * silu).astype(BF)


def ff_call(meta, x, og, wg, wu, wd, after):
    tokens, width = x.shape
    hidden = wg.shape[1]
    block = 256
    column = pl.BlockSpec((width, block), lambda j, *_: (0, j))
    return call(
        ff_kernel,
        (hidden // block,),
        [whole((tokens, width))] * 2 + [column, column, pl.BlockSpec((block, width), lambda j, *_: (j, 0))],
        [pl.BlockSpec((3, tokens, block), lambda j, *_: (0, 0, j))] + [whole((tokens, width // 2))] * 2,
        [hbm((3, tokens, hidden), BF)] + [hbm((tokens, width // 2), BF)] * 2,
        [],
        (meta, x, og, wg, wu, wd),
        48,
        after=after,
    )


def ff_back_kernel(gate, up, wg, wu, out):
    out[...] = (dot_nt(gate[0], wg[...]) + dot_nt(up[0], wu[...])).astype(BF)


def ff_back_call(planes, wg, wu):
    _, tokens, hidden = planes.shape
    width = wg.shape[0]
    block = 512
    row = pl.BlockSpec((block, hidden), lambda j: (j, 0))
    plane = lambda n: pl.BlockSpec((1, tokens, hidden), lambda j: (n, 0, 0))
    return call(
        ff_back_kernel,
        (width // block,),
        [plane(1), plane(2), row, row],
        [pl.BlockSpec((tokens, block), lambda j: (0, j))],
        [hbm((tokens, width), BF)],
        [],
        (planes, planes, wg, wu),
        40,
        prefetch=0,
    )[0]


def ff_out_kernel(hm, wd, out):
    out[...] = dot_nn(hm[0], wd[...]).astype(BF)


def ff_out_call(planes, wd):
    _, tokens, hidden = planes.shape
    width = wd.shape[1]
    block = 512
    return call(
        ff_out_kernel,
        (width // block,),
        [pl.BlockSpec((1, tokens, hidden), lambda j: (0, 0, 0)), pl.BlockSpec((hidden, block), lambda j: (0, j))],
        [pl.BlockSpec((tokens, block), lambda j: (0, j))],
        [hbm((tokens, width), BF)],
        [],
        (planes, wd),
        32,
        prefetch=0,
    )[0]


def norm_back(turned, raw, gain, cos, sin):
    upstream = turned * cos - pltpu.roll(turned, HEAD // 2, 1) * sin
    inverse = lax.rsqrt(jnp.mean(raw * raw, axis=-1, keepdims=True) + EPS)
    scaled = upstream * gain
    through = inverse * scaled - raw * (inverse * inverse * inverse) * jnp.mean(
        raw * scaled, axis=-1, keepdims=True
    )
    return through.astype(BF), jnp.sum(upstream * raw * inverse, axis=0, keepdims=True)


def attend_back_kernel(slot_count, docs, group, scale, meta, *refs):
    bg, wo, q_ref, refs = refs[0], refs[1], refs[2], refs[3:]
    keys, refs = refs[:slot_count], refs[slot_count:]
    o_ref, lse_ref, q_raw, gq, cos, sin = refs[:6]
    dq_out, even_out, odd_low, odd_high, gain_out, keep, send = refs[6:]
    r, g = pl.program_id(0), pl.program_id(1)
    first = r * slot_count
    bases = pl.num_programs(0) * slot_count

    @pl.when(g == 0)
    def _():
        half_out(bg, meta[bases + slot_count], keep, send)

    @pl.when((r == 0) & (g == 0))
    def _():
        gain_out[...] = jnp.zeros_like(gain_out)

    span = q_ref.shape[0]
    d_out = dot_nt(bg[...], wo[...]).astype(BF)
    d_out = jnp.concatenate([d_out[:, h * HEAD : (h + 1) * HEAD] for h in range(group)], axis=0)
    o_rows = stack_heads(o_ref, group)
    queries = stack_heads(q_ref, group)
    centre = jnp.sum(d_out.astype(F32) * o_rows.astype(F32), axis=-1, keepdims=True)
    lse = lse_ref[0, 0]
    high, low = bounds(meta, bases + slot_count + 1, r, docs, span, group)
    k_place = lax.broadcasted_iota(I32, (1, span), 1)
    dq = jnp.zeros((group * span, HEAD), F32)
    for s in range(slot_count):
        half = slot_count // 4
        if s % 2 == 0:
            out = even_out.at[s // 2, 0]
        else:
            out = (odd_low if s // 2 < half else odd_high).at[s // 2 % half, 0]

        def some(dq, s=s, out=out):
            raw = dot_nt(queries, keys[s][0, 0]) * (scale * LOG2E)
            place = k_place + meta[bases + s]
            probs = jnp.where((place >= low) & (place <= high), jnp.exp2(raw - lse), 0.0)
            d_probs = dot_nt(d_out, keys[s][0, 1])
            d_score = (probs * (d_probs - centre)).astype(BF)
            out[0] = (dot_tn(d_score, queries) * scale).astype(BF)
            out[1] = dot_tn(probs.astype(BF), d_out).astype(BF)
            return dq + dot_nn(d_score, keys[s][0, 0])

        def none(dq, out=out):
            out[...] = jnp.zeros(out.shape, BF)
            return dq

        dq = lax.cond(meta[first + s] > 0, some, none, dq)

    gain = gq[...]
    gain_total = jnp.zeros((1, HEAD), F32)
    for h in range(group):
        rows = dq[h * span : (h + 1) * span] * scale
        d_raw, part = norm_back(rows, q_raw[:, h * HEAD : (h + 1) * HEAD], gain, cos[...], sin[...])
        dq_out[:, h * HEAD : (h + 1) * HEAD] = d_raw
        gain_total = gain_total + part
    gain_out[...] += gain_total


def attend_back_call(meta, docs, bg, wo, queries, kv_slots, attended, lse, q_raw, gq, tables, after):
    slot_count = len(kv_slots)
    tokens, width = bg.shape
    nq = queries.shape[1]
    row_count, _, span, nk = kv_slots[0].shape
    heads, group = nk // HEAD, nq // nk
    wide = group * HEAD
    rows = pl.BlockSpec((span, wide), lambda r, g, *_: (r, g))
    by_row = lambda n: pl.BlockSpec((span, n), lambda r, g, *_: (r, 0))
    kv_out = lambda n: pl.BlockSpec((n, 1, 2, span, HEAD), lambda r, g, *_: (0, r, 0, 0, g))
    kv_shape = lambda n: hbm((n, row_count, 2, span, nk), BF)
    half, quarter = slot_count // 2, slot_count // 4
    return call(
        functools.partial(attend_back_kernel, slot_count, docs, group, HEAD**-0.5),
        (row_count, heads),
        [by_row(width), pl.BlockSpec((wide, width), lambda r, g, *_: (g, 0)), rows]
        + [pl.BlockSpec((1, 2, span, HEAD), lambda r, g, *_: (r, 0, 0, g))] * slot_count
        + [rows, pl.BlockSpec((1, 1, group * span, 1), lambda r, g, *_: (r, g, 0, 0))]
        + [rows, whole((1, HEAD)), by_row(HEAD), by_row(HEAD)],
        [rows, kv_out(half), kv_out(quarter), kv_out(quarter), whole((1, HEAD)), by_row(width // 2), by_row(width // 2)],
        [
            hbm((tokens, nq), BF),
            kv_shape(half),
            kv_shape(quarter),
            kv_shape(quarter),
            sds((1, HEAD), F32),
            hbm((tokens, width // 2), BF),
            hbm((tokens, width // 2), BF),
        ],
        [],
        (meta, bg, wo, queries, *kv_slots, attended, lse, q_raw, gq, *tables),
        40,
        after=after,
    )


def key_back_kernel(count, row_count, *refs):
    pieces, refs = refs[:count], refs[count:]
    dq_ref, k_raw, gk, cos, sin, all_out, gain_out = refs
    span, nk = pieces[0].shape[2:]
    nq = dq_ref.shape[1]
    all_out[:, :nq] = dq_ref[...]
    gain_total = jnp.zeros((1, HEAD), F32)
    for r in range(row_count):
        rows = slice(r * span, (r + 1) * span)
        for h in range(nk // HEAD):
            at = slice(h * HEAD, (h + 1) * HEAD)
            turned = sum(p[r, 0, :, at].astype(F32) for p in pieces)
            d_raw, part = norm_back(turned, k_raw[rows, at], gk[...], cos[rows], sin[rows])
            all_out[rows, nq + h * HEAD : nq + (h + 1) * HEAD] = d_raw
            gain_total = gain_total + part
        all_out[rows, nq + nk :] = sum(p[r, 1].astype(F32) for p in pieces).astype(BF)
    gain_out[...] = gain_total


def key_back_call(pieces, dq, k_raw, gk, tables, after):
    tokens, nq = dq.shape
    nk = k_raw.shape[1]
    return call(
        functools.partial(key_back_kernel, len(pieces), pieces[0].shape[0]),
        (1,),
        [whole(pieces[0].shape)] * len(pieces)
        + [whole((tokens, nq)), whole((tokens, nk)), whole((1, HEAD)), whole((tokens, HEAD)), whole((tokens, HEAD))],
        [whole((tokens, nq + 2 * nk)), whole((1, HEAD))],
        [hbm((tokens, nq + 2 * nk), BF), hbm((1, HEAD), F32)],
        [],
        (*pieces, dq, k_raw, gk, *tables),
        40,
        prefetch=0,
        after=after,
    )


def back_kernel(grads, wq, wk, wv, out):
    nq, nk = wq.shape[1], wk.shape[1]
    part = (
        dot_nt(grads[:, :nq], wq[...])
        + dot_nt(grads[:, nq : nq + nk], wk[...])
        + dot_nt(grads[:, nq + nk :], wv[...])
    )
    out[...] = part.astype(BF)


def back_call(grads, weights):
    tokens, cols = grads.shape
    width = weights[0].shape[0]
    block = width // 4
    return call(
        back_kernel,
        (4,),
        [whole((tokens, cols))] + [pl.BlockSpec((block, w.shape[1]), lambda j: (j, 0)) for w in weights],
        [pl.BlockSpec((tokens, block), lambda j: (0, j))],
        [hbm((tokens, width), BF)],
        [],
        (grads, *weights),
        40,
        prefetch=0,
    )[0]


def turn_rows(ids, parts, left_refs, turned):
    tokens, rows = left_refs[0].shape
    part = turned.shape[0] // parts
    for k, ref in enumerate(left_refs):
        for n in range(parts):
            block = ref[:, pl.ds(pl.multiple_of(ids[n] * part, HEAD), part)]
            turned[n * part : (n + 1) * part, k * tokens : (k + 1) * tokens] = block.T


def put_rows(total, outs, at):
    part = total.shape[0] // len(outs)
    for n, out in enumerate(outs):
        out[at] = total[n * part : (n + 1) * part].astype(BF)


def ff_grad_kernel(count, ids, *refs):
    lefts, p0, p1, outs, turned = refs[: 4 * count], refs[4 * count], refs[4 * count + 1], refs[4 * count + 2 : -1], refs[-1]

    @pl.when(pl.program_id(0) == 0)
    def _():
        for k in range(4):
            for n in range(count):
                block = lefts[k * count + n]
                tokens, part = block.shape
                at = k % 2 * tokens
                turned[k // 2, n * part : (n + 1) * part, at : at + tokens] = block[...].T

    for n in range(3):
        right = jnp.concatenate([p0[n], p1[n]], axis=0)
        put_rows(dot_nn(turned[min(n, 1)], right), outs, n)


def ff_grad_call(ids, ogs, xs, planes):
    tokens, rows = xs[0].shape
    hidden = planes[0].shape[2]
    wide = next(w for w in (512, 384, 256, 128) if hidden % w == 0)
    part = rows // 4
    count = ids.shape[0]
    left = lambda n: pl.BlockSpec((tokens, part), lambda c, ids: (0, ids[n]))
    return call(
        functools.partial(ff_grad_kernel, count),
        (hidden // wide,),
        [left(n) for _ in range(4) for n in range(count)]
        + [pl.BlockSpec((3, tokens, wide), lambda c, ids: (0, 0, c))] * 2,
        [pl.BlockSpec((3, part, wide), lambda c, ids: (0, 0, c))] * count,
        [hbm((3, part, hidden), BF)] * count,
        [pltpu.VMEM((2, count * part, 2 * tokens), BF)],
        (ids, *(v for v in (*ogs, *xs) for _ in range(count)), *planes),
        48,
        free=True,
    )


def attn_grad_kernel(steps, ids, x0, x1, b0, b1, g0, g1, o0, o1, *refs):
    outs, turned = refs[:-1], refs[-1]
    c = pl.program_id(0)

    @pl.when(c == 0)
    def _():
        turn_rows(ids, len(outs), (x0, x1), turned)

    @pl.when(c == steps)
    def _():
        turn_rows(ids, len(outs), (b0, b1), turned)

    @pl.when(c < steps)
    def _():
        put_rows(dot_nn(turned[...], jnp.concatenate([g0[...], g1[...]], axis=0)), outs, 0)

    @pl.when(c >= steps)
    def _():
        put_rows(dot_nn(turned[...], jnp.concatenate([o0[...], o1[...]], axis=0)), outs, 0)


def attn_grad_call(ids, xs, bs, grads, outs):
    tokens, rows = xs[0].shape
    wide = outs[0].shape[1] if grads[0].shape[1] % outs[0].shape[1] == 0 else HEAD
    steps = grads[0].shape[1] // wide
    more = outs[0].shape[1] // wide
    part = rows // 4
    count = ids.shape[0]
    cols = (steps + more) * wide
    return call(
        functools.partial(attn_grad_kernel, steps),
        (steps + more,),
        [whole((tokens, rows))] * 4
        + [pl.BlockSpec((tokens, wide), lambda c, ids: (0, jnp.minimum(c, steps - 1)))] * 2
        + [pl.BlockSpec((tokens, wide), lambda c, ids: (0, jnp.maximum(c - steps, 0)))] * 2,
        [pl.BlockSpec((1, part, wide), lambda c, ids: (0, 0, c))] * count,
        [hbm((1, part, cols), BF)] * count,
        [pltpu.VMEM((count * part, 2 * tokens), BF)],
        (ids, *(in_hbm(v) for v in (*xs, *bs, grads[0])), grads[1], *(in_hbm(v) for v in outs)),
        48,
        free=True,
    )


def split_kernel(bits, keep_a, got_a, keep_b, got_b, send_a, next_a, send_b, next_b):
    j = pl.program_id(0)

    def put(out, keep, got):
        out[...] = (keep[...].astype(F32) + got[...].astype(F32)).astype(BF)

    @pl.when(j == 0)
    def _():
        put(send_a, keep_a, got_a)
        put(send_b, keep_b, got_b)

    @pl.when(j == 1)
    def _():
        put(next_a, keep_a, got_a)
        put(next_b, keep_b, got_b)


def split_call(bits, keeps, gots, after):
    *lead, rows, cols = keeps[0].shape
    zeros = (0,) * len(lead)
    half = (*lead, rows // 2, cols)
    part = lambda f: pl.BlockSpec(half, lambda j, bits: (*zeros, jnp.where(j == 0, 1 - bits[f], bits[f]), 0))
    send_a, next_a, send_b, next_b = call(
        split_kernel,
        (2,),
        [part(0), part(0), part(1), part(1)],
        [whole(half)] * 4,
        [hbm(half, BF)] * 4,
        [],
        (bits, keeps[0], gots[0], keeps[1], gots[1]),
        40,
        after=after,
    )
    return (send_a, send_b), (next_a, next_b)


def sum_kernel(bits, *refs):
    count = (len(refs) - 2) // 2
    for f, out in enumerate(refs[2 * count :]):
        total = refs[f * count][...].astype(F32)
        for ref in refs[f * count + 1 : (f + 1) * count]:
            total = total + ref[...].astype(F32)
        out[...] = total.astype(BF)


def sum_call(bits, flows, after=()):
    rows = min(v.shape[1] for v in flows[0])
    planes, _, cols = flows[0][0].shape
    block = (planes, rows // 2, cols)

    def part(v, f):
        long = v.shape[1] > rows
        return pl.BlockSpec(block, lambda j, bits: (0, j + (2 * bits[f] if long else 0), 0))

    return call(
        sum_kernel,
        (2,),
        [part(v, f) for f, vs in enumerate(flows) for v in vs],
        [pl.BlockSpec(block, lambda j, bits: (0, j, 0))] * 2,
        [hbm((planes, rows, cols), BF)] * 2,
        [],
        (bits, *(v for f in flows for v in (*(in_hbm(k) for k in f[:-1]), f[-1]))),
        40,
        after=after,
        free=True,
    )


def half_sum_call(bits, keeps, gots):
    planes, rows, cols = keeps[0].shape
    block = (planes, rows // 4, cols)
    part = lambda f: pl.BlockSpec(block, lambda j, bits: (0, j + 2 * bits[f], 0))
    return call(
        sum_kernel,
        (2,),
        [part(0), part(0), part(1), part(1)],
        [pl.BlockSpec(block, lambda j, bits: (0, j, 0))] * 2,
        [hbm((planes, rows // 2, cols), BF)] * 2,
        [],
        (bits, keeps[0], gots[0], keeps[1], gots[1]),
        40,
        free=planes == 1,
    )


def widen_kernel(count, size, planes, turned, onto, table, *refs):
    pieces, outs = refs[: count * size * planes], refs[count * size * planes + onto :]

    def put(refs, at_row):
        rows = refs[0].shape[1]
        at_row = slice(None) if size == 1 else pl.ds(pl.multiple_of(at_row * rows, rows), rows)
        at, plane = 0, 0
        for k, out in enumerate(outs):
            wide = out.shape[0 if k in turned else 1]
            value = refs[plane][0, :, at : at + wide]
            if k in turned:
                out[:, at_row] = value.T.astype(F32)
            else:
                out[at_row, :] = value.astype(F32)
            at += wide
            if at == refs[plane].shape[2]:
                at, plane = 0, plane + 1

    for k in range(count):

        @pl.when(pl.program_id(0) == k)
        def _(k=k):
            for n in range(k * size, (k + 1) * size):
                put(pieces[n * planes : (n + 1) * planes], table[count + n])


def widen_call(blocks, spots, groups, planes, shapes, turned, onto, after):
    count, size = len(groups), len(groups[0])
    _, rows, cols = groups[0][0].shape
    place = lambda n: pl.BlockSpec((1, rows, cols), lambda j, t: (n, 0, 0), pipeline_mode=pl.Buffered(1))
    by_row = lambda s: pl.BlockSpec((size * rows, s[1]), lambda j, t: (t[j], 0))
    by_col = lambda s: pl.BlockSpec((s[0], size * rows), lambda j, t: (0, t[j]))
    return call(
        functools.partial(widen_kernel, count, size, len(planes), turned, len(onto)),
        (count,),
        [place(n) for _ in range(count * size) for n in planes] + [pl.BlockSpec(memory_space=pl.ANY)] * len(onto),
        [by_col(s) if k in turned else by_row(s) for k, s in enumerate(shapes)],
        [hbm(s, F32) for s in shapes],
        [],
        (jnp.concatenate([blocks, spots]), *(p for g in groups for p in g for _ in planes), *onto),
        56,
        after=after,
        free=True,
        aliases={1 + count * size * len(planes) + k: k for k in range(len(onto))},
    )


def hold_kernel(a, b, a_out, b_out):
    a_out[...] = a[...]
    b_out[...] = b[...]


def hold_call(values):
    planes, rows, cols = values[0].shape
    block = pl.BlockSpec((1, rows, cols), lambda j: (j, 0, 0))
    return call(
        hold_kernel,
        (planes,),
        [block] * 2,
        [block] * 2,
        [hbm(values[0].shape, BF)] * 2,
        [],
        tuple(values),
        24,
        prefetch=0,
    )


def pack_kernel(a, b, q, k, out):
    rows = a.shape[0]
    out[:rows, :] = a[...]
    out[rows : 2 * rows, :] = b[...]
    out[2 * rows : 2 * rows + 1, :] = q[...]
    out[2 * rows + 1 :, :] = k[...]


def pack_call(a, b, q, k):
    arrays = [v.reshape(-1, HEAD) for v in (a, b, q, k)]
    shape = (sum(v.shape[0] for v in arrays), HEAD)
    return call(
        pack_kernel,
        (1,),
        [whole(v.shape) for v in arrays],
        [whole(shape)],
        [hbm(shape, F32)],
        [],
        tuple(arrays),
        16,
        prefetch=0,
    )[0]


def norm_kernel(x, gain, out):
    value = x[...].astype(F32)
    inverse = lax.rsqrt(jnp.mean(value * value, axis=-1, keepdims=True) + EPS)
    out[...] = (value * inverse * gain[...]).astype(BF)


def norm_call(x, gain):
    return call(
        norm_kernel,
        (1,),
        [whole(x.shape), whole(gain.shape)],
        [whole(x.shape)],
        [hbm(x.shape, BF)],
        [],
        (x, gain),
        24,
        prefetch=0,
    )[0]


def middle_kernel(x, got, gain, middle, out):
    value = x[...].astype(F32) + got[...].astype(F32)
    inverse = lax.rsqrt(jnp.mean(value * value, axis=-1, keepdims=True) + EPS)
    middle[...] = value
    out[...] = (value * inverse * gain[...]).astype(BF)


def middle_call(x, got, gain, after):
    return call(
        middle_kernel,
        (1,),
        [whole(x.shape), whole(x.shape), whole(gain.shape)],
        [whole(x.shape)] * 2,
        [hbm(x.shape, F32), hbm(x.shape, BF)],
        [],
        (x, got, gain),
        24,
        prefetch=0,
        after=after,
    )


def norm_grad_kernel(x, got, base, gain, *outs):
    value, upstream = x[...].astype(F32), got[...].astype(F32)
    inverse = lax.rsqrt(jnp.mean(value * value, axis=-1, keepdims=True) + EPS)
    scaled = upstream * gain[...]
    through = inverse * scaled - value * (inverse * inverse * inverse) * jnp.mean(
        value * scaled, axis=-1, keepdims=True
    )
    total = base[...].astype(F32) + through
    outs[0][...] = total
    outs[1][...] = jnp.sum(upstream * value * inverse, axis=0, keepdims=True)
    if len(outs) > 2:
        outs[2][...] = total.astype(BF)


def norm_grad_call(x, got, base, gain, low, after=()):
    return call(
        norm_grad_kernel,
        (1,),
        [whole(x.shape)] * 3 + [whole(gain.shape)],
        [whole(x.shape), whole(gain.shape)] + [whole(x.shape)] * low,
        [hbm(x.shape, F32), hbm(gain.shape, F32)] + [hbm(x.shape, BF)] * low,
        [],
        (x, got, base, gain),
        24,
        prefetch=0,
        after=after,
    )


class WeightSum:
    def __init__(self, masks):
        self.flows = (masks, masks[::-1])
        seq = lax.axis_index("seq")
        self.core = seq & 1
        self.bits = [jnp.stack([(seq & m[k]) // m[k] for m in self.flows]) for k in range(len(masks))]
        base = jnp.array([0, 2], I32)
        self.send_ids, self.keep_ids = base + 1 - self.bits[0], base + self.bits[0]
        self.level = 0

    def swap_level(self, sends):
        self.gots = [swap(s, "seq", m[self.level]) for s, m in zip(sends, self.flows)]
        self.level += 1

    def begin(self, sends):
        self.swap_level(sends)

    def middle(self):
        count = len(self.flows[0])
        self.terms = [[k] for k in self.kept]
        while self.level < count:
            bits = self.bits[self.level]
            if self.level < count - 1:
                sends, kept = split_call(bits, self.kept, self.gots, ())
                self.kept = kept
            else:
                sends = half_sum_call(1 - bits, self.kept, self.gots)
                self.terms = [[k, g] for k, g in zip(self.kept, self.gots)]
            self.swap_level(sends)
        self.terms = [t + [g] for t, g in zip(self.terms, self.gots)]

    def last(self, after=()):
        parts = sum_call(self.bits[-1], self.terms, after)
        for level in range(len(self.flows[0]) - 1, 0, -1):
            gots = [swap(p, "seq", m[level]) for p, m in zip(parts, self.flows)]
            parts = [
                jnp.where(self.bits[level][f] == 0, *(jnp.concatenate(v, axis=1) for v in ((p, g), (g, p))))
                for f, (p, g) in enumerate(zip(parts, gots))
            ]
        self.parts, self.spots = parts, jnp.zeros((8,), I32)
        ends = [v for p, m in zip(parts, self.flows) for v in (p, swap(p, "seq", m[0]))]
        self.groups = [(v,) for v in (*ends, *(self.other(v) for v in ends))]
        self.soon = ends

    def other(self, value):
        return swap(value, "seq", 1)

    def last_in_pieces(self):
        self.own = sum_call(self.bits[-1], self.terms)
        self.near = [swap(p, "seq", m[1]) for p, m in zip(self.own, self.flows)]
        self.parts = [self.other(v) for v in (*self.own, *self.near)]
        self.far = [swap(p, "seq", m[0]) for p, m in zip(self.own, self.flows)]
        self.soon = [self.other(v) for v in self.far]

    def finish(self):
        last = [swap(p, "seq", m[0]) for p, m in zip(hold_call(self.near), self.flows)]
        own, other = [], []
        for f in range(2):
            own += [(self.own[f], self.near[f]), (self.far[f], last[f])]
            other += [(self.parts[f], self.parts[2 + f]), (self.soon[f], self.other(last[f]))]
        self.groups = own + other
        spots = jnp.stack([s for b in self.bits[1] for s in (b, 1 - b, b, 1 - b)])
        self.spots = jnp.concatenate([spots, spots])

    def widen(self, planes, shapes, turned, early=False, onto=(), after=()):
        blocks = jnp.stack([h for f in range(2) for h in (2 * f + self.bits[0][f], 2 * f + 1 - self.bits[0][f])])
        table = jnp.concatenate([self.core * 4 + blocks, (1 - self.core) * 4 + blocks])
        half = slice(None) if not early and not onto else slice(0 if early else 1, None, 2)
        spots = self.spots.reshape(8, -1)[half].reshape(-1)
        return widen_call(table[half], spots, self.groups[half], planes, shapes, turned, tuple(onto), after)


def halves(value, core):
    half = value.shape[1] // 2
    return (
        lax.dynamic_slice_in_dim(value, core * half, half, 1),
        lax.dynamic_slice_in_dim(value, (1 - core) * half, half, 1),
    )


def body(
    hidden_in,
    output_grad,
    document_lengths,
    attention_gain,
    query_weight,
    key_weight,
    value_weight,
    query_gain,
    key_gain,
    output_weight,
    feedforward_gain,
    gate_weight,
    up_weight,
    down_weight,
):
    ORDER.clear()
    tp, seqs = lax.axis_size("tp"), lax.axis_size("seq")
    seq_at = lax.axis_index("seq")
    core = seq_at & 1
    row_count, share, width = hidden_in.shape
    span = share * tp
    masks = tuple(1 << b for b in range(1, seqs.bit_length() - 1))

    ends = jnp.stack(
        [jnp.sum(document_lengths[:, : n + 1], axis=1) for n in range(document_lengths.shape[1])], axis=1
    )
    starts = ends - document_lengths
    docs = document_lengths.shape[1]
    places = seq_at * span + jnp.arange(span, dtype=I32)
    inside = (places[None, :, None] >= starts[:, None]) & (places[None, :, None] < ends[:, None])
    begun = jnp.sum(jnp.where(inside, starts[:, None], 0), axis=2)
    slot_seq = jnp.arange(seqs, dtype=I32) ^ seq_at
    needed = (slot_seq <= seq_at)[None] & ((slot_seq + 1)[None] * span > begun[:, :1])
    meta = jnp.concatenate(
        [needed.astype(I32).reshape(-1), slot_seq * span, core[None], places[:1], starts.reshape(-1)]
    )
    frequency = ROPE_BASE ** (-2.0 * jnp.arange(HEAD // 2, dtype=F32) / HEAD)
    angles = (places[None] - begun).reshape(-1, 1).astype(F32) * frequency
    cos, sin = jnp.cos(angles), jnp.sin(angles)
    tables = (jnp.concatenate([cos, cos], 1), jnp.concatenate([-sin, sin], 1))
    core_meta = core[None]
    q_gain, k_gain = query_gain[None], key_gain[None]
    qkv_weights = (query_weight, key_weight, value_weight)

    flat = lambda v: v.reshape(-1, width)
    hidden, upward = flat(hidden_in), flat(output_grad)
    attn_gain, ff_gain = attention_gain[None], feedforward_gain[None]
    shares = lambda v: v.reshape(row_count, share, width)
    normed1 = gather_tp(shares(norm_call(hidden, attn_gain)))
    queries, kv, q_raw, k_raw, n1_keep, n1_send = qkv_call(
        core_meta, row_count, normed1, qkv_weights, (q_gain, k_gain), tables
    )
    grads = gather_tp(output_grad)
    kv_slots = []
    for value in [kv] + [swap(kv, "seq", m) for m in range(2, seqs, 2)]:
        kv_slots += [value, swap(value, "seq", 1)]
    attended, lse, o_part = attend_call(meta, docs, queries, kv_slots, output_weight)

    def both(own, sent=None):
        return [own, swap(own if sent is None else sent, "seq", 1)]

    o_both = both(attended)
    n1_both = both(n1_keep, n1_send)
    middle, normed2 = middle_call(hidden, flat(scatter_tp(o_part, row_count)), ff_gain, (grads,))
    grads_both = both(*halves(grads, core))
    normed2 = gather_tp(shares(normed2))
    planes, n2_keep, n2_send = ff_call(
        core_meta, normed2, grads, gate_weight, up_weight, down_weight, (grads_both[1], o_both[1], n1_both[1])
    )
    planes_both, n2_both = both(planes), both(n2_keep, n2_send)
    n2_got = scatter_tp(ff_back_call(planes, gate_weight, up_weight), row_count)

    ff = WeightSum(masks)
    ff.begin(ff_grad_call(ff.send_ids, grads_both, n2_both, planes_both))
    ff.kept = ff_grad_call(ff.keep_ids, grads_both, n2_both, planes_both)
    middle_grad, ff_gain_grad, branch = norm_grad_call(middle, flat(n2_got), upward, ff_gain, True, ff.gots)
    branch = gather_tp(shares(branch))
    ff.middle()
    ff_got = scatter_tp(ff_out_call(planes, down_weight), row_count)
    in_pieces = len(masks) == 2
    if in_pieces:
        ff.last_in_pieces()
    else:
        ff.last()
    dq, even, odd_low, odd_high, q_gain_grad, b_keep, b_send = attend_back_call(
        meta,
        docs,
        branch,
        output_weight,
        queries,
        kv_slots,
        attended,
        lse,
        q_raw,
        q_gain,
        tables,
        ff.parts,
    )
    odd = [v[k] for v in (swap(odd_low, "seq", 1), swap(odd_high, "seq", 1)) for k in range(seqs // 4)]
    chip = [(even[k].astype(F32) + odd[k].astype(F32)).astype(BF) for k in range(seqs // 2)]
    pieces = [chip[0]] + [swap(chip[m // 2], "seq", m) for m in range(2, seqs, 2)]
    bg_both = both(b_keep, b_send)
    all_grad, k_gain_grad = key_back_call(pieces, dq, k_raw, k_gain, tables, (*ff.soon, ff_got, bg_both[1]))
    all_both = both(all_grad)
    n1_got = scatter_tp(back_call(all_grad, qkv_weights), row_count)
    if in_pieces:
        ff.finish()
    attn = WeightSum(masks)
    ids = jnp.concatenate([attn.send_ids, attn.keep_ids])
    parts = attn_grad_call(ids, n1_both, bg_both, all_both, o_both)
    attn.kept = parts[2:]
    attn.begin(parts[:2])
    gate_up = ((1, 2), [gate_weight.shape, up_weight.shape], ())
    down = ((0,), [down_weight.shape], (0,))
    attend = ((0,), [w.shape for w in (*qkv_weights, output_weight)], (3,))
    gate_up_out, down_out = ff.widen(*gate_up, early=True), ff.widen(*down, early=True)
    attn.middle()
    input_grad, attn_gain_grad = norm_grad_call(hidden, flat(n1_got), middle_grad, attn_gain, False)
    input_grad = shares(input_grad)
    block_out = shares((middle + flat(ff_got).astype(F32)).astype(BF))
    gate_out, up_out = ff.widen(*gate_up, onto=gate_up_out)
    attn.last()
    (down_out,) = ff.widen(*down, onto=down_out)
    gains = pack_call(attn_gain_grad, ff_gain_grad, q_gain_grad, k_gain_grad)
    gains = sum_copies(gains, "tp", [1 << level for level in range(tp.bit_length() - 1)])
    for level in range(seqs.bit_length() - 1):
        gains = sum_copies(gains, "seq", [1 << level])
    query_out, key_out, value_out, output_out = attn.widen(*attend)
    gains = gains.reshape(-1)
    return (
        block_out,
        input_grad,
        gains[:width],
        query_out,
        key_out,
        value_out,
        gains[2 * width : 2 * width + HEAD],
        gains[2 * width + HEAD :],
        output_out,
        gains[width : 2 * width],
        gate_out,
        up_out,
        down_out,
    )


def solution(mesh):
    tokens, columns, rows = P(None, ("seq", "tp"), None), P(None, "tp"), P("tp", None)
    in_specs = (
        tokens,
        tokens,
        P(),
        P(),
        columns,
        columns,
        columns,
        P(),
        P(),
        rows,
        P(),
        columns,
        columns,
        rows,
    )
    out_specs = (
        tokens,
        tokens,
        P(),
        columns,
        columns,
        columns,
        P(),
        P(),
        rows,
        P(),
        columns,
        columns,
        rows,
    )
    return jax.shard_map(body, mesh=mesh, in_specs=in_specs, out_specs=out_specs, check_vma=False)
```
